128 devices in a mesh: dp: 8 (over z, y_lo), expert: 16 (over x, y_hi, core).
Axes of the slice: x: 4, y: 4 (y_hi: 2, y_lo: 2; y = y_hi * 2 + y_lo), z: 4, core: 2. Of those that a mesh axis runs over, the one named last changes fastest.
Arguments:
- tokens: bfloat16 [16384, 3584], P(('dp', 'expert')), may hold values from -6 to 6
- cotangent: bfloat16 [16384, 3584], P(('dp', 'expert')), may hold values from -6 to 6
- expert_ids: int32 [16384, 1], P(('dp', 'expert')), may hold values from 0 to 3; in each aligned block of 128 rows (0 to 127, 128 to 255, ...) at most 48 rows name the same one
- gate_scale: float32 [16384], P(('dp', 'expert')), may hold values from 0.3 to 3
- old_place: int32 [16], replicated, may hold values from 0 to 15, as said below
- new_place: int32 [16], replicated, may hold values from 0 to 15, as said below
- gate_up: bfloat16 [16, 3584, 2, 256], P('expert', 'dp'), may hold values from -0.09375 to 0.09375
- down_proj: bfloat16 [16, 256, 3584], P('expert', 'dp'), may hold values from -0.1875 to 0.1875
- first_gu: float32 [16, 3584, 2, 256], P('expert', 'dp'), may hold values from -4 to 4
- second_gu: float32 [16, 3584, 2, 256], P('expert', 'dp'), may hold values from 0.05 to 1
- first_down: float32 [16, 256, 3584], P('expert', 'dp'), may hold values from -4 to 4
- second_down: float32 [16, 256, 3584], P('expert', 'dp'), may hold values from 0.05 to 1
Outputs:
- output: bfloat16 [16384, 3584], P(('dp', 'expert'))
- token_grad: bfloat16 [16384, 3584], P(('dp', 'expert'))
- gate_up_new: bfloat16 [16, 3584, 2, 256], P('expert', 'dp')
- down_new: bfloat16 [16, 256, 3584], P('expert', 'dp')
- first_gu_new: float32 [16, 3584, 2, 256], P('expert', 'dp')
- second_gu_new: float32 [16, 3584, 2, 256], P('expert', 'dp')
- first_down_new: float32 [16, 256, 3584], P('expert', 'dp')
- second_down_new: float32 [16, 256, 3584], P('expert', 'dp')
The draws below stay inside these ranges and needn't reach their ends.
Inputs may be any that keep to these rules, and one draw needn't show every extreme that they name: `old_place`: A permutation: every piece 0 to 15 is held by exactly one index. `new_place`: A permutation equal to old_place except that two distinct experts exchange their indices slice for slice: exactly 8 entries differ. `expert_ids`: within the rows of one device no expert is named more than 48 times, a bound that some block reaches.
All inputs are finite; a program needn't handle non-finite values.
Results may differ from the reference program's by a relative error of at most 0.015.
Values may be sent and summed in bfloat16 or wider, within the bound.
No kernel may reach another device: no remote copies, remote signals or barrier semaphores. Data moves between devices by JAX's collectives and lax.ppermute only.
A program may use at most 128 MiB of HBM per device.

```python
import math
import jax
import jax.numpy as jnp
import numpy as np
from jax import lax

D = 3584
HID = 1024
HSPLIT = 4
TOPK = 1
TOK_DEV = 128
HS = 256
EXPERTS = 4
CAP = 48
TOKENS = 16384
N_DP = 8
N_EXPERT = 16


def placement_pair(key):
    pieces_all = EXPERTS * HSPLIT
    order = jax.random.permutation(jax.random.fold_in(key, 11), pieces_all).astype(jnp.int32)
    first_pick = jax.random.randint(jax.random.fold_in(key, 12), (), 0, EXPERTS)
    second_pick = (first_pick + 1 + jax.random.randint(jax.random.fold_in(key, 13), (), 0, EXPERTS - 1)) % EXPERTS
    expert_of = order // HSPLIT
    slice_of = order % HSPLIT
    swapped = jnp.where(expert_of == first_pick, second_pick * HSPLIT + slice_of, jnp.where(expert_of == second_pick, first_pick * HSPLIT + slice_of, order))
    return (order, swapped.astype(jnp.int32))


def draw_old_place(key, part):
    shared = placement_pair(key)
    return shared[0]


def draw_new_place(key, part):
    shared = placement_pair(key)
    return shared[1]


def shared_amplitude():
    return min(1.0, 0.4)


def column_ramp(low_end):
    position = jnp.arange(D, dtype=jnp.float32) / float(D - 1)
    return low_end + position


def draw_tokens(key, part):
    key = jax.random.fold_in(key, 3)
    amplitude = shared_amplitude()
    direction = jax.random.normal(jax.random.fold_in(key, 1), (D,), jnp.float32)
    noise = jax.random.normal(jax.random.fold_in(key, 2), (TOKENS, D), jnp.float32)
    values = (noise + amplitude * direction[None, :]) * column_ramp(0.5)[None, :]
    return jnp.clip(values, -6.0, 6.0).astype(jnp.bfloat16)


def draw_cotangent(key, part):
    key = jax.random.fold_in(key, 5)
    amplitude = shared_amplitude()
    direction = jax.random.normal(jax.random.fold_in(key, 1), (D,), jnp.float32)
    noise = jax.random.normal(jax.random.fold_in(key, 2), (TOKENS, D), jnp.float32)
    values = noise + amplitude * direction[None, :]
    return jnp.clip(values, -6.0, 6.0).astype(jnp.bfloat16)


def shard_levels(rng, dims, pieces, low, high):
    def one(axis_at, blocks):
        heights = jax.random.uniform(jax.random.fold_in(jax.random.fold_in(rng, 6), axis_at), (blocks,), jnp.float32, low / len(pieces), high / len(pieces))
        return jnp.repeat(jnp.exp(heights), dims[axis_at] // blocks).reshape((-1,) + (1,) * (len(dims) - axis_at - 1))

    factor_of = one(*pieces[0])
    for cut in pieces[1:]:
        factor_of = factor_of * one(*cut)
    return factor_of


def routed_block(own_key, own, number, rows, amount, top, reach, skew):
    sequence = jax.random.permutation(own_key, amount)
    heavy_load, usual = load_shares(amount, rows * top, reach, skew, True), load_shares(amount, rows * top, reach, skew, False)
    places = jnp.arange(amount)

    def named(sizes, offset_by):
        used = int((sizes > 0).sum())
        fixed = max(1, used // 4)
        moved = fixed + (places - fixed + offset_by * (used - fixed)) % max(1, amount - fixed)
        return jnp.zeros((amount,), jnp.int32).at[sequence[jnp.where(places < fixed, places, moved)]].set(jnp.asarray(sizes, jnp.int32))

    sizes = jnp.where(number % 4 == 0, named(heavy_load, number // 4), named(usual, number - number // 4 - 1))
    mixed = jax.random.permutation(jax.random.fold_in(own, 3), amount)
    donor, taker = mixed[0:amount // 2 * 2:2], mixed[1:amount // 2 * 2:2]
    room = jnp.minimum(sizes[donor] - 1, reach - sizes[taker]) // 2
    room = jnp.where((donor == sequence[0]) | (taker == sequence[0]) | (sizes[taker] == 0), 0, jnp.maximum(room, 0))
    moved = jax.random.randint(jax.random.fold_in(own, 4), (amount // 2,), 0, 1 << 20) % (room + 1)
    sizes = sizes.at[donor].add(-moved).at[taker].add(moved)
    labels = jnp.searchsorted(jnp.cumsum(sizes), jnp.arange(rows * top), side="right").astype(jnp.int32)
    listing = labels.reshape(top, rows).T
    listing = listing[jax.random.permutation(jax.random.fold_in(own, 1), rows)]
    offset_by = jax.random.randint(jax.random.fold_in(own, 2), (rows, 1), 0, top)
    return jnp.take_along_axis(listing, (jnp.arange(top)[None, :] + offset_by) % top, axis=1)


def load_shares(count, total, most, skew, full):
    weights = [(1 << 20) // math.isqrt(grade ** skew) + 1 for grade in range(1, count + 1)]
    largest = most if full else min(most, max(-(-total // count), total * weights[0] // sum(weights)))
    least = 1 if total - largest >= count - 1 else 0
    holding, surplus = [largest] + [least] * (count - 1), total - largest - least * (count - 1)
    while surplus > 0:
        movable = [i for i in range(1, count) if holding[i] < largest] or [i for i in range(1, count) if holding[i] < most]
        whole, budget = sum([weights[i] for i in movable]), surplus
        for i in movable:
            addition = min(most - holding[i], max(1, budget * weights[i] // whole), surplus)
            holding[i] = holding[i] + addition
            surplus = surplus - addition
    return np.array(holding)


def scatter_about(key, dims, width, reach, cuts=(), kind=jnp.bfloat16):
    result = width * jax.random.normal(key, dims, jnp.float32)
    if cuts:
        result = result * shard_levels(key, dims, cuts, -0.22, 0.18)
    return jnp.clip(result, -reach, reach).astype(kind)


def setup_inputs(seed: int = 0) -> dict:
    key_of = jax.random.split(jax.random.key(seed), 13)
    tokens = draw_tokens(jax.random.fold_in(key_of[12], 71), 0)
    cotangent = draw_cotangent(jax.random.fold_in(key_of[12], 71), 0)
    expert_ids_keys = jax.random.split(jax.random.fold_in(key_of[2], 1), TOKENS // TOK_DEV)
    expert_ids_turns = jax.random.permutation(jax.random.fold_in(key_of[2], 3), TOKENS // TOK_DEV)
    expert_ids = jax.vmap(lambda own, number: routed_block(jax.random.fold_in(key_of[2], 2), own, number, TOK_DEV, EXPERTS, TOPK, CAP, 2))(expert_ids_keys, expert_ids_turns).reshape((TOKENS, TOPK))
    gate_scale = jnp.clip(jnp.exp(math.log(3.0) - 2.3025851 * jax.random.uniform(key_of[3], (TOKENS,), jnp.float32) ** shard_levels(key_of[3], (TOKENS,), ((0, 128),), -0.2, 0.2)), 0.3, 3.0)
    old_place = draw_old_place(jax.random.fold_in(key_of[12], 71), 0)
    new_place = draw_new_place(jax.random.fold_in(key_of[12], 71), 0)
    gate_up = scatter_about(key_of[6], (N_EXPERT, D, 2, HS), D ** -0.5, 0.09375, ((0, 16), (1, 8)))
    down_proj = scatter_about(key_of[7], (N_EXPERT, HS, D), HID ** -0.5, 0.1875, ((0, 16), (1, 8)))
    first_gu = scatter_about(key_of[8], (N_EXPERT, D, 2, HS), 0.3, 4.0, ((0, 16), (1, 8)), jnp.float32)
    second_gu = jnp.clip(jnp.exp(math.log(1.0) - 2.9957323 * jax.random.uniform(key_of[9], (N_EXPERT, D, 2, HS), jnp.float32) ** shard_levels(key_of[9], (N_EXPERT, D, 2, HS), ((0, 16), (1, 8)), -0.2, 0.2)), 0.05, 1.0)
    first_down = scatter_about(key_of[10], (N_EXPERT, HS, D), 0.3, 4.0, ((0, 16), (1, 8)), jnp.float32)
    second_down = jnp.clip(jnp.exp(math.log(1.0) - 2.9957323 * jax.random.uniform(key_of[11], (N_EXPERT, HS, D), jnp.float32) ** shard_levels(key_of[11], (N_EXPERT, HS, D), ((0, 16), (1, 8)), -0.2, 0.2)), 0.05, 1.0)
    return dict(tokens=tokens, cotangent=cotangent, expert_ids=expert_ids, gate_scale=gate_scale, old_place=old_place, new_place=new_place, gate_up=gate_up, down_proj=down_proj, first_gu=first_gu, second_gu=second_gu, first_down=first_down, second_down=second_down)


first_decay = 0.9
second_decay = 0.95
learn_rate = 0.001
adam_epsilon = 1e-08

def swish_parts(gate_half):
    sigmoid_val = jax.nn.sigmoid(gate_half)
    return (gate_half * sigmoid_val, sigmoid_val * (1.0 + gate_half * (1.0 - sigmoid_val)))

def adam_update(weight, first_mom, second_mom, grad, clip_factor):
    scaled_grad = clip_factor * grad
    first_next = first_decay * first_mom + (1.0 - first_decay) * scaled_grad
    second_next = second_decay * second_mom + (1.0 - second_decay) * scaled_grad * scaled_grad
    weight_next = weight.astype(jnp.float32) - learn_rate * first_next / (jnp.sqrt(second_next) + adam_epsilon)
    return (weight_next.astype(jnp.bfloat16), first_next, second_next)

def expert_pass(row_block, cot_block, gu_piece, down_piece):
    w_pair = gu_piece.astype(jnp.float32)
    w_down = down_piece.astype(jnp.float32)
    hidden = jnp.einsum('rd,sdkh->rskh', row_block.astype(jnp.float32), w_pair)
    gate_half = hidden[:, :, 0]
    up_half = hidden[:, :, 1]
    swish, slope = swish_parts(gate_half)
    activation = (swish * up_half).astype(jnp.bfloat16)
    partial_value = jnp.einsum('rsh,shd->rsd', activation.astype(jnp.float32), w_down).astype(jnp.bfloat16)
    combined = lax.optimization_barrier(jnp.sum(partial_value.astype(jnp.float32), axis=1))
    back = jnp.einsum('rd,shd->rsh', cot_block.astype(jnp.float32), w_down)
    dgu = jnp.stack([back * up_half * slope, back * swish], axis=2).astype(jnp.bfloat16)
    grad_down = jnp.einsum('rsh,rd->shd', activation.astype(jnp.float32), cot_block.astype(jnp.float32))
    grad_pair = jnp.einsum('rd,rskh->sdkh', row_block.astype(jnp.float32), dgu.astype(jnp.float32))
    token_part = jnp.einsum('rskh,sdkh->rsd', dgu.astype(jnp.float32), w_pair).astype(jnp.bfloat16)
    token_sum = lax.optimization_barrier(jnp.sum(token_part.astype(jnp.float32), axis=1))
    return (combined, token_sum, grad_pair, grad_down)

def reference(tokens, cotangent, expert_ids, gate_scale, old_place, new_place, gate_up, down_proj, first_gu, second_gu, first_down, second_down):
    numbers = jnp.arange(N_EXPERT, dtype=jnp.int32)
    holder = jnp.zeros((N_EXPERT,), jnp.int32).at[old_place].set(numbers)
    piece_gu = gate_up[holder].reshape(EXPERTS, HSPLIT, D, 2, HS)
    piece_down = down_proj[holder].reshape(EXPERTS, HSPLIT, HS, D)
    scaled = (gate_scale[:, None] * cotangent.astype(jnp.float32)).astype(jnp.bfloat16)
    group_rows = N_EXPERT * TOK_DEV
    lane_total = N_EXPERT * CAP

    def group_pass(carry, data):
        token_block, cot_group, route_group = data

        def one_expert(expert):
            route_mask = route_group == expert
            row_index = jnp.nonzero(route_mask, size=lane_total, fill_value=0)[0].astype(jnp.int32)
            valid_rows = (jnp.arange(lane_total) < jnp.sum(route_mask)).astype(jnp.bfloat16)[:, None]
            row_block = token_block[row_index] * valid_rows
            cot_block = cot_group[row_index] * valid_rows
            gu_piece = lax.dynamic_index_in_dim(piece_gu, expert, 0, keepdims=False)
            down_piece = lax.dynamic_index_in_dim(piece_down, expert, 0, keepdims=False)
            combined, token_sum, grad_pair, grad_down = expert_pass(row_block, cot_block, gu_piece, down_piece)
            weight_rows = valid_rows.astype(jnp.float32)
            return (row_index, combined * weight_rows, token_sum * weight_rows, grad_pair, grad_down)
        row_index, combined, token_sum, grad_pair, grad_down = lax.map(one_expert, jnp.arange(EXPERTS, dtype=jnp.int32))
        flat_index = row_index.reshape(-1)
        out_group = jnp.zeros((group_rows, D), jnp.float32).at[flat_index].add(combined.reshape(-1, D))
        grad_group = jnp.zeros((group_rows, D), jnp.float32).at[flat_index].add(token_sum.reshape(-1, D))
        sum_pair, sum_down = carry
        sum_pair = sum_pair + lax.optimization_barrier(grad_pair.astype(jnp.bfloat16)).astype(jnp.float32)
        sum_down = sum_down + lax.optimization_barrier(grad_down.astype(jnp.bfloat16)).astype(jnp.float32)
        return ((sum_pair, sum_down), (out_group, grad_group))
    start = (jnp.zeros((EXPERTS, HSPLIT, D, 2, HS), jnp.float32), jnp.zeros((EXPERTS, HSPLIT, HS, D), jnp.float32))
    data = (tokens.reshape(N_DP, group_rows, D), scaled.reshape(N_DP, group_rows, D), expert_ids[:, 0].reshape(N_DP, group_rows))
    (sum_pair, sum_down), (out_all, grad_all) = lax.scan(group_pass, start, data)
    output = (gate_scale[:, None] * out_all.reshape(TOKENS, D)).astype(jnp.bfloat16)
    token_grad = grad_all.reshape(TOKENS, D).astype(jnp.bfloat16)
    grad_pair = sum_pair.reshape(N_EXPERT, D, 2, HS)
    grad_down = sum_down.reshape(N_EXPERT, HS, D)
    total = jnp.sum(grad_pair * grad_pair) + jnp.sum(grad_down * grad_down)
    limit = 0.5 * jnp.sqrt(jnp.float32(3 * N_EXPERT * D * HS))
    clip_factor = jnp.minimum(1.0, limit / (jnp.sqrt(total) + 1e-06))
    gu_next, first_gu_next, second_gu_next = adam_update(gate_up[holder], first_gu[holder], second_gu[holder], grad_pair, clip_factor)
    down_next, first_down_next, second_down_next = adam_update(down_proj[holder], first_down[holder], second_down[holder], grad_down, clip_factor)
    return (output, token_grad, gu_next[new_place], down_next[new_place], first_gu_next[new_place], second_gu_next[new_place], first_down_next[new_place], second_down_next[new_place])
```

```python
import jax
import jax.numpy as jnp
from jax import lax
from jax.experimental import pallas as pl
from jax.experimental.pallas import tpu as pltpu
from jax.sharding import PartitionSpec as P

HSPLIT = 4
PIECES = 16
DP = 8
GU_ROWS = 448
DOWN_ROWS = 32
DOWN_BLOCKS = 7
PACK_ROWS = GU_ROWS + DOWN_ROWS * DOWN_BLOCKS
PACK_COLS = 512
KERNEL_VMEM = 32 * 1024 * 1024

first_decay = 0.9
second_decay = 0.95
learn_rate = 0.001
adam_epsilon = 1e-08

X_GROUPS = [[x * 4 + s for x in range(4)] for s in range(4)]
CORE_SWAP = [(i, i ^ 1) for i in range(16)]
YHI_SWAP = [(i, i ^ 2) for i in range(16)]


def dp_shift(dz, dy):
    return [(z * 2 + y, ((z + dz) % 4) * 2 + (y ^ dy)) for z in range(4) for y in range(2)]


def pack(gu, down):
    rows = down.reshape(DOWN_ROWS, DOWN_BLOCKS, PACK_COLS).transpose(1, 0, 2)
    return jnp.concatenate([gu.reshape(GU_ROWS, PACK_COLS), rows.reshape(-1, PACK_COLS)], axis=0)


def unpack(packed):
    gu = packed[:GU_ROWS].reshape(1, GU_ROWS, 2, 256)
    down = packed[GU_ROWS:].reshape(DOWN_BLOCKS, DOWN_ROWS, PACK_COLS).transpose(1, 0, 2)
    return gu, down.reshape(1, DOWN_ROWS, -1)


def to_parts(packed):
    rows = packed.shape[0] // 4
    return packed.reshape(4, rows, 4, 128).transpose(0, 2, 1, 3).reshape(PIECES, rows, 128)


def from_parts(parts):
    rows = parts.shape[1]
    return parts.reshape(4, 4, rows, 128).transpose(0, 2, 1, 3).reshape(4 * rows, PACK_COLS)


def spread(parts):
    return lax.all_to_all(parts, "expert", split_axis=0, concat_axis=0, tiled=True)


def assemble_kernel(*refs):
    shards, (gu_ref, down_ref) = refs[:DP], refs[DP:]
    me = lax.axis_index("dp")
    z, y = me // 2, lax.rem(me, 2)
    for k, shard in enumerate(shards):
        src = lax.rem(z + 4 - k // 2, 4) * 2 + lax.rem(y + k % 2, 2)
        gu_rows = pl.ds(pl.multiple_of(src * GU_ROWS, GU_ROWS), GU_ROWS)
        down_rows = pl.ds(pl.multiple_of(src * DOWN_ROWS, DOWN_ROWS), DOWN_ROWS)
        gu_ref[gu_rows, :] = shard[:GU_ROWS, :]
        for n in range(DOWN_BLOCKS):
            at = GU_ROWS + n * DOWN_ROWS
            down_ref[down_rows, n * PACK_COLS : (n + 1) * PACK_COLS] = shard[at : at + DOWN_ROWS, :]


def assemble(shards, width, hidden_width):
    return pl.pallas_call(
        assemble_kernel,
        out_shape=(
            jax.ShapeDtypeStruct((width, PACK_COLS), jnp.bfloat16),
            jax.ShapeDtypeStruct((hidden_width, width), jnp.bfloat16),
        ),
        in_specs=[pl.BlockSpec(memory_space=pltpu.VMEM)] * DP,
        out_specs=(pl.BlockSpec(memory_space=pltpu.VMEM),) * 2,
        compiler_params=pltpu.CompilerParams(vmem_limit_bytes=KERNEL_VMEM),
        name="assemble",
    )(*shards)


def split_kernel(gu_ref, down_ref, *shards):
    me = lax.axis_index("dp")
    z, y = me // 2, lax.rem(me, 2)
    for k, shard in enumerate(shards):
        dst = lax.rem(z + k // 2, 4) * 2 + lax.rem(y + k % 2, 2)
        gu_rows = pl.ds(pl.multiple_of(dst * GU_ROWS, GU_ROWS), GU_ROWS)
        down_rows = pl.ds(pl.multiple_of(dst * DOWN_ROWS, DOWN_ROWS), DOWN_ROWS)
        shard[:GU_ROWS, :] = gu_ref[gu_rows, :]
        for n in range(DOWN_BLOCKS):
            at = GU_ROWS + n * DOWN_ROWS
            shard[at : at + DOWN_ROWS, :] = down_ref[down_rows, n * PACK_COLS : (n + 1) * PACK_COLS]


def split(grad_pair, grad_down):
    return pl.pallas_call(
        split_kernel,
        out_shape=(jax.ShapeDtypeStruct((PACK_ROWS, PACK_COLS), jnp.bfloat16),) * DP,
        in_specs=[pl.BlockSpec(memory_space=pltpu.VMEM)] * 2,
        out_specs=(pl.BlockSpec(memory_space=pltpu.VMEM),) * DP,
        compiler_params=pltpu.CompilerParams(vmem_limit_bytes=KERNEL_VMEM),
        name="split",
    )(grad_pair, grad_down)


def gather_dp(shard):
    partner = lax.ppermute(shard, "dp", dp_shift(0, 1))
    mine = [lax.ppermute(shard, "dp", dp_shift(dz, 0)) for dz in (1, 3, 2)]
    theirs = [lax.ppermute(partner, "dp", dp_shift(dz, 0)) for dz in (1, 3, 2)]
    return shard, partner, mine[0], theirs[0], mine[2], theirs[2], mine[1], theirs[1]


def reduce_dp(chunks):
    def along_z(dy):
        got = [lax.ppermute(chunks[2 * dz + dy], "dp", dp_shift(dz, 0)) for dz in (1, 3, 2)]
        total = chunks[dy].astype(jnp.float32)
        for term in got:
            total = total + term.astype(jnp.float32)
        return total

    other = lax.ppermute(along_z(1).astype(jnp.bfloat16), "dp", dp_shift(0, 1))
    return along_z(0) + other.astype(jnp.float32)


def per_device(
    tokens,
    cotangent,
    expert_ids,
    gate_scale,
    old_place,
    new_place,
    gate_up,
    down_proj,
    first_gu,
    second_gu,
    first_down,
    second_down,
):
    experts = PIECES // HSPLIT
    tok_rows, width = tokens.shape
    hidden_width = down_proj.shape[1] * DP
    capacity = 3 * tok_rows // (2 * experts)
    numbers = jnp.arange(PIECES, dtype=jnp.int32)
    old_holder = jnp.sum(
        (old_place[None, :] == numbers[:, None]).astype(jnp.int32) * numbers[None, :], axis=1
    )
    source = old_holder[new_place]

    weight_parts = spread(to_parts(pack(gate_up, down_proj)))
    shard = from_parts(spread(weight_parts[old_holder]))
    gu_full, down_full = assemble(gather_dp(shard), width, hidden_width)

    chosen = expert_ids[:, 0]
    hit_table = (chosen[:, None] == jnp.arange(experts, dtype=jnp.int32)[None, :]).astype(jnp.int32)
    rank_in = jnp.sum((jnp.cumsum(hit_table, axis=0) - 1) * hit_table, axis=1)
    lane_code = chosen * capacity + rank_in
    lanes = jnp.arange(experts * capacity, dtype=jnp.int32)
    picker = (lanes[:, None] == lane_code[None, :]).astype(jnp.bfloat16)

    def send_rows(row_data):
        lined_up = jnp.dot(picker, row_data, preferred_element_type=jnp.float32).astype(
            jnp.bfloat16
        )
        own = lax.all_to_all(
            lined_up.reshape(experts, capacity, width),
            "expert",
            split_axis=0,
            concat_axis=0,
            axis_index_groups=X_GROUPS,
            tiled=True,
        ).reshape(-1, width)
        over_y = lax.ppermute(own, "expert", YHI_SWAP)
        return jnp.concatenate(
            [
                own,
                over_y,
                lax.ppermute(own, "expert", CORE_SWAP),
                lax.ppermute(over_y, "expert", CORE_SWAP),
            ],
            axis=0,
        )

    def return_rows(partial_value):
        half, quarter = partial_value.shape[0] // 2, partial_value.shape[0] // 4
        other = lax.ppermute(partial_value[half:], "expert", CORE_SWAP)
        pair = partial_value[:half].astype(jnp.float32) + other.astype(jnp.float32)
        far = lax.ppermute(pair[quarter:].astype(jnp.bfloat16), "expert", YHI_SWAP)
        own = (pair[:quarter] + far.astype(jnp.float32)).astype(jnp.bfloat16)
        back_home = lax.all_to_all(
            own.reshape(experts, capacity, width),
            "expert",
            split_axis=0,
            concat_axis=0,
            axis_index_groups=X_GROUPS,
            tiled=True,
        ).reshape(-1, width)
        return lax.dot_general(
            picker, back_home, (((0,), (0,)), ((), ())), preferred_element_type=jnp.float32
        )

    scaled = (gate_scale[:, None] * cotangent.astype(jnp.float32)).astype(jnp.bfloat16)
    row_block = send_rows(tokens)
    cot_block = send_rows(scaled)

    hidden = jnp.dot(row_block, gu_full, preferred_element_type=jnp.float32)
    gate_half = hidden[:, :hidden_width]
    up_half = hidden[:, hidden_width:]
    sigmoid_val = jax.nn.sigmoid(gate_half)
    swish = gate_half * sigmoid_val
    activation = (swish * up_half).astype(jnp.bfloat16)
    back = lax.dot_general(
        cot_block, down_full, (((1,), (1,)), ((), ())), preferred_element_type=jnp.float32
    )
    slope = sigmoid_val * (1.0 + gate_half * (1.0 - sigmoid_val))
    dgu = jnp.concatenate([back * up_half * slope, back * swish], axis=1).astype(jnp.bfloat16)
    grad_down = lax.dot_general(
        activation, cot_block, (((0,), (0,)), ((), ())), preferred_element_type=jnp.float32
    ).astype(jnp.bfloat16)
    grad_pair = lax.dot_general(
        row_block, dgu, (((0,), (0,)), ((), ())), preferred_element_type=jnp.float32
    ).astype(jnp.bfloat16)
    grad = reduce_dp(split(grad_pair, grad_down))

    partial_value = jnp.dot(activation, down_full, preferred_element_type=jnp.float32).astype(
        jnp.bfloat16
    )
    output = (return_rows(partial_value) * gate_scale[:, None]).astype(jnp.bfloat16)
    token_part = lax.dot_general(
        dgu, gu_full, (((1,), (1,)), ((), ())), preferred_element_type=jnp.float32
    ).astype(jnp.bfloat16)
    token_grad = return_rows(token_part).astype(jnp.bfloat16)

    moments = jnp.concatenate(
        [
            to_parts(pack(first_gu, first_down).astype(jnp.bfloat16)),
            to_parts(pack(second_gu, second_down).astype(jnp.bfloat16)),
        ],
        axis=1,
    )
    state = spread(jnp.concatenate([weight_parts, spread(moments)], axis=1)[source])
    rows = PACK_ROWS // 4
    weight_now = from_parts(state[:, :rows]).astype(jnp.float32)
    first_now = from_parts(state[:, rows : 2 * rows]).astype(jnp.float32)
    second_now = from_parts(state[:, 2 * rows :]).astype(jnp.float32)

    local_squares = jnp.sum(grad * grad)
    total = jnp.sum(
        lax.all_to_all(
            jnp.broadcast_to(local_squares, (DP * PIECES, 128)),
            ("dp", "expert"),
            split_axis=0,
            concat_axis=0,
            tiled=True,
        )[:, 0]
    )
    limit = 0.5 * jnp.sqrt(jnp.float32(3 * PIECES * width * hidden_width))
    clip_factor = jnp.minimum(1.0, limit / (jnp.sqrt(total) + 1e-06))

    grad_parts = spread(to_parts(grad.astype(jnp.bfloat16)))
    grad_now = from_parts(spread(grad_parts[new_place])).astype(jnp.float32)
    scaled_grad = clip_factor * grad_now
    first_next = first_decay * first_now + (1.0 - first_decay) * scaled_grad
    second_next = second_decay * second_now + (1.0 - second_decay) * scaled_grad * scaled_grad
    weight_next = weight_now - learn_rate * first_next / (jnp.sqrt(second_next) + adam_epsilon)
    gu_next, down_next = unpack(weight_next.astype(jnp.bfloat16))
    first_gu_next, first_down_next = unpack(first_next)
    second_gu_next, second_down_next = unpack(second_next)
    return (
        output,
        token_grad,
        gu_next,
        down_next,
        first_gu_next,
        second_gu_next,
        first_down_next,
        second_down_next,
    )


def solution(mesh):
    rows = P(("dp", "expert"), None)
    gu, down = P("expert", "dp", None, None), P("expert", "dp", None)
    return jax.shard_map(
        per_device,
        mesh=mesh,
        in_specs=(rows, rows, rows, P(("dp", "expert")), P(), P(), gu, down, gu, gu, down, down),
        out_specs=(rows, rows, gu, down, gu, gu, down, down),
        check_vma=False,
    )
```

```python
import jax
import jax.numpy as jnp
from jax import lax
from jax.experimental import pallas as pl
from jax.experimental.pallas import tpu as pltpu
from jax.sharding import PartitionSpec as P

HSPLIT = 4
PIECES = 16
DP = 8
GU_ROWS = 448
DOWN_ROWS = 32
DOWN_BLOCKS = 7
PACK_ROWS = GU_ROWS + DOWN_ROWS * DOWN_BLOCKS
PACK_COLS = 512
KERNEL_VMEM = 32 * 1024 * 1024

first_decay = 0.9
second_decay = 0.95
learn_rate = 0.001
adam_epsilon = 1e-08

CORE_SWAP = [(i, i ^ 1) for i in range(16)]
YHI_SWAP = [(i, i ^ 2) for i in range(16)]


X_GROUPS = [[x * 4 + s for x in range(4)] for s in range(4)]


def x_shift(dx):
    return [(x * 4 + s, ((x + dx) % 4) * 4 + s) for x in range(4) for s in range(4)]


def dp_shift(dz, dy):
    return [(z * 2 + y, ((z + dz) % 4) * 2 + (y ^ dy)) for z in range(4) for y in range(2)]


def dp_flip(dz, dy):
    return [(i, i ^ (dz * 2 + dy)) for i in range(DP)]


def after(value, *earlier):
    return lax.optimization_barrier((value, *earlier))[0]


def pack(gu, down):
    rows = down.reshape(DOWN_ROWS, DOWN_BLOCKS, PACK_COLS).transpose(1, 0, 2)
    return jnp.concatenate([gu.reshape(GU_ROWS, PACK_COLS), rows.reshape(-1, PACK_COLS)], axis=0)


def unpack(packed):
    gu = packed[:GU_ROWS].reshape(1, GU_ROWS, 2, 256)
    down = packed[GU_ROWS:].reshape(DOWN_BLOCKS, DOWN_ROWS, PACK_COLS).transpose(1, 0, 2)
    return gu, down.reshape(1, DOWN_ROWS, -1)


def to_parts(packed):
    rows = packed.shape[0] // 4
    return packed.reshape(4, rows, 4, 128).transpose(0, 2, 1, 3).reshape(PIECES, rows, 128)


def from_parts(parts):
    rows = parts.shape[1]
    return parts.reshape(4, 4, rows, 128).transpose(0, 2, 1, 3).reshape(4 * rows, PACK_COLS)


def spread(parts):
    return lax.all_to_all(parts, "expert", split_axis=0, concat_axis=0, tiled=True)


def assemble_kernel(own, below, above, far_same, far_other, gu_ref, down_ref):
    me = lax.axis_index("dp")
    z, y = me // 2, lax.rem(me, 2)
    shards = [(0, own, 0), (0, own, 1), (3, below, 0), (3, below, 1), (1, above, 0), (1, above, 1)]
    shards += [(2, far_same, 0), (2, far_other, 1)]
    for dz, ref, dy in shards:
        shard = ref if dz == 2 else ref.at[dy]
        src = lax.rem(z + dz, 4) * 2 + lax.rem(y + dy, 2)
        gu_rows = pl.ds(pl.multiple_of(src * GU_ROWS, GU_ROWS), GU_ROWS)
        down_rows = pl.ds(pl.multiple_of(src * DOWN_ROWS, DOWN_ROWS), DOWN_ROWS)
        gu_ref[gu_rows, :] = shard[:GU_ROWS, :]
        for n in range(DOWN_BLOCKS):
            at = GU_ROWS + n * DOWN_ROWS
            down_ref[down_rows, n * PACK_COLS : (n + 1) * PACK_COLS] = shard[at : at + DOWN_ROWS, :]


def gather_dp(shard, width, hidden_width):
    partner = lax.ppermute(shard, "dp", dp_shift(0, 1))
    own = jnp.stack([shard, partner])
    below = lax.ppermute(own, "dp", dp_shift(1, 0))
    above = lax.ppermute(own, "dp", dp_shift(3, 0))
    far_same = lax.ppermute(below[0], "dp", dp_shift(1, 0))
    far_other = lax.ppermute(above[1], "dp", dp_shift(3, 0))
    return pl.pallas_call(
        assemble_kernel,
        out_shape=(
            jax.ShapeDtypeStruct((width, PACK_COLS), jnp.bfloat16),
            jax.ShapeDtypeStruct((hidden_width, width), jnp.bfloat16),
        ),
        in_specs=[pl.BlockSpec(memory_space=pltpu.VMEM)] * 5,
        out_specs=(pl.BlockSpec(memory_space=pltpu.VMEM),) * 2,
        compiler_params=pltpu.CompilerParams(vmem_limit_bytes=KERNEL_VMEM),
        name="assemble",
    )(own, below, above, far_same, far_other)


def split_kernel(gu_ref, down_ref, own, above, below, far_same, far_other):
    me = lax.axis_index("dp")
    z, y = me // 2, lax.rem(me, 2)
    shards = [(0, own, 0), (0, own, 1), (1, above, 0), (1, above, 1), (3, below, 0), (3, below, 1)]
    shards += [(2, far_same, 0), (2, far_other, 1)]
    for dz, ref, dy in shards:
        shard = ref if dz == 2 else ref.at[dy]
        dst = lax.rem(z + dz, 4) * 2 + lax.rem(y + dy, 2)
        gu_rows = pl.ds(pl.multiple_of(dst * GU_ROWS, GU_ROWS), GU_ROWS)
        down_rows = pl.ds(pl.multiple_of(dst * DOWN_ROWS, DOWN_ROWS), DOWN_ROWS)
        shard[:GU_ROWS, :] = gu_ref[gu_rows, :]
        for n in range(DOWN_BLOCKS):
            at = GU_ROWS + n * DOWN_ROWS
            shard[at : at + DOWN_ROWS, :] = down_ref[down_rows, n * PACK_COLS : (n + 1) * PACK_COLS]


def split(grad_pair, grad_down):
    one = jax.ShapeDtypeStruct((PACK_ROWS, PACK_COLS), jnp.bfloat16)
    two = jax.ShapeDtypeStruct((2, PACK_ROWS, PACK_COLS), jnp.bfloat16)
    return pl.pallas_call(
        split_kernel,
        out_shape=(two, two, two, one, one),
        in_specs=[pl.BlockSpec(memory_space=pltpu.VMEM)] * 2,
        out_specs=(pl.BlockSpec(memory_space=pltpu.VMEM),) * 5,
        compiler_params=pltpu.CompilerParams(vmem_limit_bytes=KERNEL_VMEM),
        name="split",
    )(grad_pair, grad_down)


def add(term, other):
    return term.astype(jnp.float32) + other.astype(jnp.float32)


def per_device(
    tokens,
    cotangent,
    expert_ids,
    gate_scale,
    old_place,
    new_place,
    gate_up,
    down_proj,
    first_gu,
    second_gu,
    first_down,
    second_down,
):
    experts = PIECES // HSPLIT
    tok_rows, width = tokens.shape
    hidden_width = down_proj.shape[1] * DP
    capacity = 3 * tok_rows // (2 * experts)
    numbers = jnp.arange(PIECES, dtype=jnp.int32)
    old_holder = jnp.sum(
        (old_place[None, :] == numbers[:, None]).astype(jnp.int32) * numbers[None, :], axis=1
    )
    source = old_holder[new_place]

    moments = jnp.concatenate(
        [
            to_parts(pack(first_gu, first_down).astype(jnp.bfloat16)),
            to_parts(pack(second_gu, second_down).astype(jnp.bfloat16)),
        ],
        axis=1,
    )
    weight_parts = spread(to_parts(pack(gate_up, down_proj)))
    shard = from_parts(spread(after(weight_parts, moments)[old_holder]))
    gu_full, down_full = gather_dp(shard, width, hidden_width)

    chosen = expert_ids[:, 0]
    hit_table = (chosen[:, None] == jnp.arange(experts, dtype=jnp.int32)[None, :]).astype(jnp.int32)
    rank_in = jnp.sum((jnp.cumsum(hit_table, axis=0) - 1) * hit_table, axis=1)
    own_x = lax.axis_index("expert") // HSPLIT
    steps = (own_x - jnp.arange(experts, dtype=jnp.int32)) % experts
    lanes = jnp.arange(experts * capacity, dtype=jnp.int32)
    lane_code = ((chosen - own_x) % experts) * capacity + rank_in
    picker = (lanes[:, None] == lane_code[None, :]).astype(jnp.bfloat16)
    expert_code = chosen * capacity + rank_in
    expert_picker = (lanes[:, None] == expert_code[None, :]).astype(jnp.bfloat16)

    def pick(table, row_data):
        lined_up = jnp.dot(table, row_data, preferred_element_type=jnp.float32)
        return lined_up.astype(jnp.bfloat16).reshape(experts, capacity, width)

    def along_x(blocks, sign):
        moved = [
            lax.ppermute(blocks[k], "expert", x_shift(sign * k)) for k in range(1, experts)
        ]
        return jnp.concatenate([blocks[0], *moved], axis=0)

    def to_slices(own):
        over_y = lax.ppermute(own, "expert", YHI_SWAP)
        return (
            own,
            over_y,
            lax.ppermute(own, "expert", CORE_SWAP),
            lax.ppermute(over_y, "expert", CORE_SWAP),
        )

    def over_core(own_half, other_half):
        quarter = own_half.shape[0] // 2
        other = lax.ppermute(other_half, "expert", CORE_SWAP)
        far = own_half[quarter:].astype(jnp.float32) + other[quarter:].astype(jnp.float32)
        near = own_half[:quarter].astype(jnp.float32) + other[:quarter].astype(jnp.float32)
        return near, far.astype(jnp.bfloat16)

    def over_yhi(near, far):
        return (near + lax.ppermute(far, "expert", YHI_SWAP).astype(jnp.float32)).astype(
            jnp.bfloat16
        )

    def to_home(own):
        back_home = along_x(own.reshape(experts, capacity, width), -1)
        return lax.dot_general(
            picker, back_home, (((0,), (0,)), ((), ())), preferred_element_type=jnp.float32
        )

    scaled = (gate_scale[:, None] * cotangent.astype(jnp.float32)).astype(jnp.bfloat16)
    row_block = jnp.concatenate(to_slices(along_x(pick(picker, tokens), 1)), axis=0)
    cot_lanes = lax.all_to_all(
        pick(expert_picker, after(scaled, weight_parts)),
        "expert",
        split_axis=0,
        concat_axis=0,
        axis_index_groups=X_GROUPS,
        tiled=True,
    )
    cot_rows = to_slices(cot_lanes[steps].reshape(-1, width))
    cot_block = jnp.concatenate(cot_rows, axis=0)

    hidden = jnp.dot(row_block, gu_full, preferred_element_type=jnp.float32)
    gate_half = hidden[:, :hidden_width]
    up_half = hidden[:, hidden_width:]
    sigmoid_val = jax.nn.sigmoid(gate_half)
    swish = gate_half * sigmoid_val
    activation = (swish * up_half).astype(jnp.bfloat16)
    back = lax.dot_general(
        cot_block, down_full, (((1,), (1,)), ((), ())), preferred_element_type=jnp.float32
    )
    slope = sigmoid_val * (1.0 + gate_half * (1.0 - sigmoid_val))
    dgu = jnp.concatenate([back * up_half * slope, back * swish], axis=1).astype(jnp.bfloat16)
    grad_down = lax.dot_general(
        activation, cot_block, (((0,), (0,)), ((), ())), preferred_element_type=jnp.float32
    ).astype(jnp.bfloat16)
    grad_pair = lax.dot_general(
        row_block, dgu, (((0,), (0,)), ((), ())), preferred_element_type=jnp.float32
    ).astype(jnp.bfloat16)
    own, above, below, far_same, far_other, activation, dgu = lax.optimization_barrier(
        (*split(grad_pair, grad_down), activation, dgu)
    )
    half = activation.shape[0] // 2

    def down_rows(rows):
        return jnp.dot(rows, down_full, preferred_element_type=jnp.float32).astype(jnp.bfloat16)

    def token_rows(rows):
        return lax.dot_general(
            rows, gu_full, (((1,), (1,)), ((), ())), preferred_element_type=jnp.float32
        ).astype(jnp.bfloat16)

    out_near, out_far = over_core(down_rows(activation[:half]), down_rows(activation[half:]))
    far_same = lax.ppermute(far_same, "dp", dp_shift(1, 0))
    far_other = lax.ppermute(far_other, "dp", dp_shift(3, 0))
    above = jnp.stack([add(above[0], far_same).astype(jnp.bfloat16), above[1]])
    below = jnp.stack([below[0], add(below[1], far_other).astype(jnp.bfloat16)])
    above, below = after(above, out_far), after(below, out_far)
    above = lax.ppermute(above, "dp", dp_shift(1, 0))
    below = lax.ppermute(below, "dp", dp_shift(3, 0))
    out_rows = over_yhi(out_near, out_far)
    token_near, token_far = over_core(token_rows(dgu[:half]), token_rows(dgu[half:]))
    other_sum = (add(own[1], above[1]) + below[1].astype(jnp.float32)).astype(jnp.bfloat16)
    other_sum = lax.ppermute(after(other_sum, token_far), "dp", dp_shift(0, 1))
    grad = add(own[0], above[0]) + add(below[0], other_sum)
    grad = after(grad, out_rows)
    own_token_rows = over_yhi(token_near, token_far)
    output = (to_home(out_rows) * gate_scale[:, None]).astype(jnp.bfloat16)
    token_grad = to_home(own_token_rows).astype(jnp.bfloat16)

    moments = spread(after(moments, cot_rows[1]))
    state = spread(jnp.concatenate([weight_parts, moments], axis=1)[source])
    rows = PACK_ROWS // 4
    weight_now = from_parts(state[:, :rows]).astype(jnp.float32)
    first_now = from_parts(state[:, rows : 2 * rows]).astype(jnp.float32)
    second_now = from_parts(state[:, 2 * rows :]).astype(jnp.float32)

    squares = jnp.sum(grad * grad)
    digits = []
    for _ in range(3):
        digit = lax.reduce_precision(squares, 8, 7)
        digits.append(digit)
        squares = squares - digit
    digits = jnp.broadcast_to(jnp.stack(digits + [jnp.float32(0.0)] * 5)[None, :, None], (PIECES, 8, 128))
    grad_parts = spread(
        jnp.concatenate(
            [to_parts(grad.astype(jnp.bfloat16)), digits.astype(jnp.bfloat16)], axis=1
        )
    )
    grad_now = from_parts(spread(grad_parts[new_place, :rows])).astype(jnp.float32)
    total = jnp.sum(grad_parts[:, rows : rows + 3, 0].astype(jnp.float32))
    for step in ((0, 1), (1, 0), (2, 0)):
        total = total + lax.ppermute(total, "dp", dp_flip(*step))
    limit = 0.5 * jnp.sqrt(jnp.float32(3 * PIECES * width * hidden_width))
    clip_factor = jnp.minimum(1.0, limit / (jnp.sqrt(total) + 1e-06))

    scaled_grad = clip_factor * grad_now
    first_next = first_decay * first_now + (1.0 - first_decay) * scaled_grad
    second_next = second_decay * second_now + (1.0 - second_decay) * scaled_grad * scaled_grad
    weight_next = weight_now - learn_rate * first_next / (jnp.sqrt(second_next) + adam_epsilon)
    gu_next, down_next = unpack(weight_next.astype(jnp.bfloat16))
    first_gu_next, first_down_next = unpack(first_next)
    second_gu_next, second_down_next = unpack(second_next)
    return (
        output,
        token_grad,
        gu_next,
        down_next,
        first_gu_next,
        second_gu_next,
        first_down_next,
        second_down_next,
    )


def solution(mesh):
    rows = P(("dp", "expert"), None)
    gu, down = P("expert", "dp", None, None), P("expert", "dp", None)
    return jax.shard_map(
        per_device,
        mesh=mesh,
        in_specs=(rows, rows, rows, P(("dp", "expert")), P(), P(), gu, down, gu, gu, down, down),
        out_specs=(rows, rows, gu, down, gu, gu, down, down),
        check_vma=False,
    )
```

```python
import jax
import jax.numpy as jnp
from jax import lax
from jax.experimental import pallas as pl
from jax.experimental.pallas import tpu as pltpu
from jax.sharding import PartitionSpec as P

HSPLIT = 4
PIECES = 16
DP = 8
GU_ROWS = 448
DOWN_ROWS = 32
DOWN_BLOCKS = 7
PACK_ROWS = GU_ROWS + DOWN_ROWS * DOWN_BLOCKS
PACK_COLS = 512
KERNEL_VMEM = 32 * 1024 * 1024

first_decay = 0.9
second_decay = 0.95
learn_rate = 0.001
adam_epsilon = 1e-08

CORE_SWAP = [(i, i ^ 1) for i in range(16)]
YHI_SWAP = [(i, i ^ 2) for i in range(16)]


X_GROUPS = [[x * 4 + s for x in range(4)] for s in range(4)]


def x_shift(dx):
    return [(x * 4 + s, ((x + dx) % 4) * 4 + s) for x in range(4) for s in range(4)]


def dp_shift(dz, dy):
    return [(z * 2 + y, ((z + dz) % 4) * 2 + (y ^ dy)) for z in range(4) for y in range(2)]


def dp_flip(dz, dy):
    return [(i, i ^ (dz * 2 + dy)) for i in range(DP)]


def after(value, *earlier):
    return lax.optimization_barrier((value, *earlier))[0]


def pack(gu, down):
    rows = down.reshape(DOWN_ROWS, DOWN_BLOCKS, PACK_COLS).transpose(1, 0, 2)
    return jnp.concatenate([gu.reshape(GU_ROWS, PACK_COLS), rows.reshape(-1, PACK_COLS)], axis=0)


def unpack(packed):
    gu = packed[:GU_ROWS].reshape(1, GU_ROWS, 2, 256)
    down = packed[GU_ROWS:].reshape(DOWN_BLOCKS, DOWN_ROWS, PACK_COLS).transpose(1, 0, 2)
    return gu, down.reshape(1, DOWN_ROWS, -1)


def to_parts(packed):
    rows = packed.shape[0] // 4
    return packed.reshape(4, rows, 4, 128).transpose(0, 2, 1, 3).reshape(PIECES, rows, 128)


def from_parts(parts):
    rows = parts.shape[1]
    return parts.reshape(4, 4, rows, 128).transpose(0, 2, 1, 3).reshape(4 * rows, PACK_COLS)


def spread(parts):
    return lax.all_to_all(parts, "expert", split_axis=0, concat_axis=0, tiled=True)


def assemble_kernel(own, below, above, far_same, far_other, gu_ref, down_ref):
    me = lax.axis_index("dp")
    z, y = me // 2, lax.rem(me, 2)
    shards = [(0, own, 0), (0, own, 1), (3, below, 0), (3, below, 1), (1, above, 0), (1, above, 1)]
    shards += [(2, far_same, 0), (2, far_other, 1)]
    for dz, ref, dy in shards:
        shard = ref if dz == 2 else ref.at[dy]
        src = lax.rem(z + dz, 4) * 2 + lax.rem(y + dy, 2)
        gu_rows = pl.ds(pl.multiple_of(src * GU_ROWS, GU_ROWS), GU_ROWS)
        down_rows = pl.ds(pl.multiple_of(src * DOWN_ROWS, DOWN_ROWS), DOWN_ROWS)
        gu_ref[gu_rows, :] = shard[:GU_ROWS, :]
        for n in range(DOWN_BLOCKS):
            at = GU_ROWS + n * DOWN_ROWS
            down_ref[down_rows, n * PACK_COLS : (n + 1) * PACK_COLS] = shard[at : at + DOWN_ROWS, :]


def first_steps(shard):
    partner = lax.ppermute(shard, "dp", dp_shift(0, 1))
    own = jnp.stack([shard, partner])
    below = lax.ppermute(own, "dp", dp_shift(1, 0))
    above = lax.ppermute(own, "dp", dp_shift(3, 0))
    return own, below, above


def gather_dp(own, below, above, width, hidden_width):
    far_same = lax.ppermute(below[0], "dp", dp_shift(1, 0))
    far_other = lax.ppermute(above[1], "dp", dp_shift(3, 0))
    full = pl.pallas_call(
        assemble_kernel,
        out_shape=(
            jax.ShapeDtypeStruct((width, PACK_COLS), jnp.bfloat16),
            jax.ShapeDtypeStruct((hidden_width, width), jnp.bfloat16),
        ),
        in_specs=[pl.BlockSpec(memory_space=pltpu.VMEM)] * 5,
        out_specs=(pl.BlockSpec(memory_space=pltpu.VMEM),) * 2,
        compiler_params=pltpu.CompilerParams(vmem_limit_bytes=KERNEL_VMEM),
        name="assemble",
    )(own, below, above, far_same, far_other)
    return (*full, far_same, far_other)


def split_kernel(gu_ref, down_ref, own, above, below, far_same, far_other):
    me = lax.axis_index("dp")
    z, y = me // 2, lax.rem(me, 2)
    shards = [(0, own, 0), (0, own, 1), (1, above, 0), (1, above, 1), (3, below, 0), (3, below, 1)]
    shards += [(2, far_same, 0), (2, far_other, 1)]
    for dz, ref, dy in shards:
        shard = ref if dz == 2 else ref.at[dy]
        dst = lax.rem(z + dz, 4) * 2 + lax.rem(y + dy, 2)
        gu_rows = pl.ds(pl.multiple_of(dst * GU_ROWS, GU_ROWS), GU_ROWS)
        down_rows = pl.ds(pl.multiple_of(dst * DOWN_ROWS, DOWN_ROWS), DOWN_ROWS)
        shard[:GU_ROWS, :] = gu_ref[gu_rows, :]
        for n in range(DOWN_BLOCKS):
            at = GU_ROWS + n * DOWN_ROWS
            shard[at : at + DOWN_ROWS, :] = down_ref[down_rows, n * PACK_COLS : (n + 1) * PACK_COLS]


def split(grad_pair, grad_down):
    one = jax.ShapeDtypeStruct((PACK_ROWS, PACK_COLS), jnp.bfloat16)
    two = jax.ShapeDtypeStruct((2, PACK_ROWS, PACK_COLS), jnp.bfloat16)
    return pl.pallas_call(
        split_kernel,
        out_shape=(two, two, two, one, one),
        in_specs=[pl.BlockSpec(memory_space=pltpu.VMEM)] * 2,
        out_specs=(pl.BlockSpec(memory_space=pltpu.VMEM),) * 5,
        compiler_params=pltpu.CompilerParams(vmem_limit_bytes=KERNEL_VMEM),
        name="split",
    )(grad_pair, grad_down)


def add(term, other):
    return term.astype(jnp.float32) + other.astype(jnp.float32)


def join_kernel(above, below, far_same, far_other, above_out, below_out):
    for at in range(0, PACK_ROWS, 32):
        here = pl.ds(at, 32)
        above_out[0, here, :] = add(above[0, here, :], far_same[here, :]).astype(jnp.bfloat16)
        above_out[1, here, :] = above[1, here, :]
        below_out[0, here, :] = below[0, here, :]
        below_out[1, here, :] = add(below[1, here, :], far_other[here, :]).astype(jnp.bfloat16)


def join(above, below, far_same, far_other):
    return pl.pallas_call(
        join_kernel,
        out_shape=(jax.ShapeDtypeStruct(above.shape, above.dtype),) * 2,
        in_specs=[pl.BlockSpec(memory_space=pltpu.VMEM)] * 4,
        out_specs=(pl.BlockSpec(memory_space=pltpu.VMEM),) * 2,
        compiler_params=pltpu.CompilerParams(vmem_limit_bytes=KERNEL_VMEM),
        name="join",
    )(above, below, far_same, far_other)


def finish_kernel(own, above, below, other, parts, squares_out, total):
    rows = PACK_ROWS // 4
    squares = jnp.zeros((8, PACK_COLS), jnp.float32)
    for at in range(0, PACK_ROWS, 32):
        here = pl.ds(at, 32)
        value = add(own[0, here, :], above[0, here, :]) + add(below[0, here, :], other[here, :])
        total[here, :] = value
        squares = squares + jnp.sum((value * value).reshape(4, 8, PACK_COLS), axis=0)
    squares_out[...] = jnp.broadcast_to(jnp.sum(squares, keepdims=True), (8, 128))
    pad = jnp.zeros((8, 128), jnp.float32)
    for k in range(PIECES):
        value = total[pl.ds(k // 4 * rows, rows), pl.ds(k % 4 * 128, 128)]
        parts[k] = jnp.concatenate([value, pad], axis=0).astype(jnp.bfloat16)


def finish(own, above, below, other):
    return pl.pallas_call(
        finish_kernel,
        out_shape=(
            jax.ShapeDtypeStruct((PIECES, PACK_ROWS // 4 + 8, 128), jnp.bfloat16),
            jax.ShapeDtypeStruct((8, 128), jnp.float32),
        ),
        in_specs=[pl.BlockSpec(memory_space=pltpu.VMEM)] * 4,
        out_specs=(pl.BlockSpec(memory_space=pltpu.VMEM),) * 2,
        scratch_shapes=[pltpu.VMEM((PACK_ROWS, PACK_COLS), jnp.float32)],
        compiler_params=pltpu.CompilerParams(vmem_limit_bytes=KERNEL_VMEM),
        name="finish",
    )(own, above, below, other)


def regroup_kernel(place, parts, squares, out):
    left = squares[0:1, :]
    digits = []
    for _ in range(3):
        digit = left.astype(jnp.bfloat16).astype(jnp.float32)
        digits.append(digit)
        left = left - digit
    row = lax.broadcasted_iota(jnp.int32, (8, 128), 0)
    digits = jnp.where(row == 0, digits[0], jnp.where(row == 1, digits[1], digits[2]))
    for k in range(PIECES):
        value = parts[place[k]].astype(jnp.float32)[: PACK_ROWS // 4]
        out[k] = jnp.concatenate([value, digits], axis=0).astype(jnp.bfloat16)


def regroup(place, parts, squares):
    return pl.pallas_call(
        regroup_kernel,
        out_shape=jax.ShapeDtypeStruct(parts.shape, parts.dtype),
        in_specs=[
            pl.BlockSpec(memory_space=pltpu.SMEM),
            pl.BlockSpec(memory_space=pltpu.VMEM),
            pl.BlockSpec(memory_space=pltpu.VMEM),
        ],
        out_specs=pl.BlockSpec(memory_space=pltpu.VMEM),
        compiler_params=pltpu.CompilerParams(vmem_limit_bytes=KERNEL_VMEM),
        name="regroup",
    )(place, parts, squares)


def per_device(
    tokens,
    cotangent,
    expert_ids,
    gate_scale,
    old_place,
    new_place,
    gate_up,
    down_proj,
    first_gu,
    second_gu,
    first_down,
    second_down,
):
    experts = PIECES // HSPLIT
    tok_rows, width = tokens.shape
    hidden_width = down_proj.shape[1] * DP
    capacity = 3 * tok_rows // (2 * experts)
    numbers = jnp.arange(PIECES, dtype=jnp.int32)
    old_holder = jnp.sum(
        (old_place[None, :] == numbers[:, None]).astype(jnp.int32) * numbers[None, :], axis=1
    )
    source = old_holder[new_place]

    moments = jnp.concatenate(
        [
            to_parts(pack(first_gu, first_down).astype(jnp.bfloat16)),
            to_parts(pack(second_gu, second_down).astype(jnp.bfloat16)),
        ],
        axis=1,
    )
    weight_parts = spread(to_parts(pack(gate_up, down_proj)))
    shard = from_parts(spread(after(weight_parts, moments)[old_holder]))
    shards = first_steps(shard)

    chosen = expert_ids[:, 0]
    chosen = jnp.stack([chosen, lax.ppermute(chosen, "expert", YHI_SWAP)])
    hit_table = (chosen[:, :, None] == jnp.arange(experts, dtype=jnp.int32)).astype(jnp.int32)
    rank_in = jnp.sum((jnp.cumsum(hit_table, axis=1) - 1) * hit_table, axis=2)
    own_x = lax.axis_index("expert") // HSPLIT
    steps = (own_x - jnp.arange(experts, dtype=jnp.int32)) % experts

    def picker_of(codes, count):
        lanes = jnp.arange(count, dtype=jnp.int32)
        return (lanes[:, None] == codes.reshape(-1)[None, :]).astype(jnp.bfloat16)

    block = (chosen - own_x) % experts
    picker = picker_of(block[0] * capacity + rank_in[0], experts * capacity)
    expert_picker = picker_of(chosen[0] * capacity + rank_in[0], experts * capacity)
    halves = jnp.arange(2, dtype=jnp.int32)[:, None] * capacity
    home_picker = picker_of(block * 2 * capacity + halves + rank_in, experts * 2 * capacity)

    def pick(table, row_data):
        lined_up = jnp.dot(table, row_data, preferred_element_type=jnp.float32)
        return lined_up.astype(jnp.bfloat16).reshape(experts, capacity, width)

    def along_x(blocks, sign, *earlier):
        moved = [
            lax.ppermute(blocks[k], "expert", x_shift(sign * k)) for k in range(1, experts)
        ]
        moved = lax.optimization_barrier((*moved, *earlier))[: len(moved)]
        return jnp.concatenate([blocks[0], *moved], axis=0)

    def over_x(blocks):
        return lax.all_to_all(
            blocks, "expert", split_axis=0, concat_axis=0, axis_index_groups=X_GROUPS, tiled=True
        )

    def to_slices(own, *earlier):
        over_y = after(lax.ppermute(own, "expert", YHI_SWAP), *earlier)
        return (
            own,
            over_y,
            lax.ppermute(own, "expert", CORE_SWAP),
            lax.ppermute(over_y, "expert", CORE_SWAP),
        )

    def over_core(own_half, other_half):
        rows = add(own_half, lax.ppermute(other_half, "expert", CORE_SWAP)).astype(jnp.bfloat16)
        rows = rows.reshape(2, experts, capacity, width).transpose(1, 0, 2, 3)
        return rows.reshape(experts, 2 * capacity, width)

    def home_steps(blocks):
        moved = [lax.ppermute(blocks[k], "expert", x_shift(-k)) for k in range(1, experts)]
        return blocks[0], *moved

    def unpick(blocks):
        both = lax.dot_general(
            home_picker,
            jnp.concatenate(blocks, axis=0),
            (((0,), (0,)), ((), ())),
            preferred_element_type=jnp.float32,
        )
        theirs = lax.ppermute(both[tok_rows:].astype(jnp.bfloat16), "expert", YHI_SWAP)
        return both[:tok_rows], theirs

    scaled = (gate_scale[:, None] * cotangent.astype(jnp.float32)).astype(jnp.bfloat16)
    token_own = along_x(pick(picker, tokens), 1, shard)
    row_block = jnp.concatenate(to_slices(token_own), axis=0)
    cot_lanes = over_x(after(pick(expert_picker, scaled), shard))
    *shards, cot_lanes = lax.optimization_barrier((*shards, cot_lanes))
    gu_full, down_full, *last_steps = gather_dp(*shards, width, hidden_width)
    cot_rows = to_slices(cot_lanes[steps].reshape(-1, width), *last_steps)
    cot_block = jnp.concatenate(cot_rows, axis=0)
    moments = spread(after(moments, cot_rows[1]))

    hidden = jnp.dot(row_block, gu_full, preferred_element_type=jnp.float32)
    gate_half = hidden[:, :hidden_width]
    up_half = hidden[:, hidden_width:]
    sigmoid_val = jax.nn.sigmoid(gate_half)
    swish = gate_half * sigmoid_val
    activation = (swish * up_half).astype(jnp.bfloat16)
    back = lax.dot_general(
        cot_block, down_full, (((1,), (1,)), ((), ())), preferred_element_type=jnp.float32
    )
    slope = sigmoid_val * (1.0 + gate_half * (1.0 - sigmoid_val))
    dgu = jnp.concatenate([back * up_half * slope, back * swish], axis=1).astype(jnp.bfloat16)
    half = activation.shape[0] // 2

    def down_rows(rows):
        return jnp.dot(rows, down_full, preferred_element_type=jnp.float32).astype(jnp.bfloat16)

    def token_rows(rows):
        return lax.dot_general(
            rows, gu_full, (((1,), (1,)), ((), ())), preferred_element_type=jnp.float32
        ).astype(jnp.bfloat16)

    out_other, out_own = down_rows(activation[half:]), down_rows(activation[:half])
    dgu, out_other, out_own = lax.optimization_barrier((dgu, out_other, out_own))
    out_blocks = over_core(out_own, out_other)
    grad_down = lax.dot_general(
        activation, cot_block, (((0,), (0,)), ((), ())), preferred_element_type=jnp.float32
    ).astype(jnp.bfloat16)
    grad_pair = lax.dot_general(
        row_block, dgu, (((0,), (0,)), ((), ())), preferred_element_type=jnp.float32
    ).astype(jnp.bfloat16)
    own, above, below, far_same, far_other, dgu, moments = lax.optimization_barrier(
        (*split(grad_pair, grad_down), dgu, moments)
    )
    far_same = lax.ppermute(far_same, "dp", dp_shift(1, 0))
    far_other = lax.ppermute(far_other, "dp", dp_shift(3, 0))
    above, below = join(above, below, far_same, far_other)
    above, below, dgu, moments = lax.optimization_barrier((above, below, dgu, moments))
    above = lax.ppermute(above, "dp", dp_shift(1, 0))
    below = lax.ppermute(below, "dp", dp_shift(3, 0))
    state = spread(jnp.concatenate([weight_parts, moments], axis=1)[source])
    token_blocks = over_core(token_rows(dgu[:half]), token_rows(dgu[half:]))
    other_sum = (add(own[1], above[1]) + below[1].astype(jnp.float32)).astype(jnp.bfloat16)
    other_sum, out_blocks, token_blocks, state = lax.optimization_barrier(
        (other_sum, out_blocks, token_blocks, state)
    )
    out_back, token_back = home_steps(out_blocks), home_steps(token_blocks)
    other_sum = lax.ppermute(other_sum, "dp", dp_shift(0, 1))
    grad_parts, squares = finish(own, above, below, other_sum)
    rows = PACK_ROWS // 4
    weight_now = from_parts(state[:, :rows]).astype(jnp.float32)
    first_now = from_parts(state[:, rows : 2 * rows]).astype(jnp.float32)
    second_now = from_parts(state[:, 2 * rows :]).astype(jnp.float32)

    for step in ((1, 0), (2, 0), (0, 1)):
        squares = squares + lax.ppermute(squares, "dp", dp_flip(*step))
    out_home, out_theirs = unpick(lax.optimization_barrier((*out_back, squares))[:experts])
    grad_parts = spread(grad_parts)
    token_back = lax.optimization_barrier((*token_back, grad_parts))[:experts]
    token_home, token_theirs = unpick(token_back)
    grad_parts = spread(regroup(new_place, grad_parts, squares))
    grad_now = from_parts(grad_parts[:, :rows]).astype(jnp.float32)
    total = jnp.sum(grad_parts[:, rows : rows + 3, 0].astype(jnp.float32))
    limit = 0.5 * jnp.sqrt(jnp.float32(3 * PIECES * width * hidden_width))
    clip_factor = jnp.minimum(1.0, limit / (jnp.sqrt(total) + 1e-06))

    output = (add(out_home, out_theirs) * gate_scale[:, None]).astype(jnp.bfloat16)
    token_grad = add(token_home, token_theirs).astype(jnp.bfloat16)

    scaled_grad = clip_factor * grad_now
    first_next = first_decay * first_now + (1.0 - first_decay) * scaled_grad
    second_next = second_decay * second_now + (1.0 - second_decay) * scaled_grad * scaled_grad
    weight_next = weight_now - learn_rate * first_next / (jnp.sqrt(second_next) + adam_epsilon)
    gu_next, down_next = unpack(weight_next.astype(jnp.bfloat16))
    first_gu_next, first_down_next = unpack(first_next)
    second_gu_next, second_down_next = unpack(second_next)
    return (
        output,
        token_grad,
        gu_next,
        down_next,
        first_gu_next,
        second_gu_next,
        first_down_next,
        second_down_next,
    )


def solution(mesh):
    rows = P(("dp", "expert"), None)
    gu, down = P("expert", "dp", None, None), P("expert", "dp", None)
    return jax.shard_map(
        per_device,
        mesh=mesh,
        in_specs=(rows, rows, rows, P(("dp", "expert")), P(), P(), gu, down, gu, gu, down, down),
        out_specs=(rows, rows, gu, down, gu, gu, down, down),
        check_vma=False,
    )
```

```python
import jax
import jax.numpy as jnp
from jax import lax
from jax.experimental import pallas as pl
from jax.experimental.pallas import tpu as pltpu
from jax.sharding import PartitionSpec as P

HSPLIT = 4
PIECES = 16
DP = 8
GU_ROWS = 448
DOWN_ROWS = 32
DOWN_BLOCKS = 7
PACK_ROWS = GU_ROWS + DOWN_ROWS * DOWN_BLOCKS
PACK_COLS = 512
KERNEL_VMEM = 32 * 1024 * 1024

first_decay = 0.9
second_decay = 0.95
learn_rate = 0.001
adam_epsilon = 1e-08

CORE_SWAP = [(i, i ^ 1) for i in range(16)]
YHI_SWAP = [(i, i ^ 2) for i in range(16)]


X_GROUPS = [[x * 4 + s for x in range(4)] for s in range(4)]


def x_shift(dx):
    return [(x * 4 + s, ((x + dx) % 4) * 4 + s) for x in range(4) for s in range(4)]


def dp_shift(dz, dy):
    return [(z * 2 + y, ((z + dz) % 4) * 2 + (y ^ dy)) for z in range(4) for y in range(2)]


def dp_flip(dz, dy):
    return [(i, i ^ (dz * 2 + dy)) for i in range(DP)]


def after(value, *earlier):
    return lax.optimization_barrier((value, *earlier))[0]


def pack(gu, down):
    rows = down.reshape(DOWN_ROWS, DOWN_BLOCKS, PACK_COLS).transpose(1, 0, 2)
    return jnp.concatenate([gu.reshape(GU_ROWS, PACK_COLS), rows.reshape(-1, PACK_COLS)], axis=0)


def unpack(packed):
    gu = packed[:GU_ROWS].reshape(1, GU_ROWS, 2, 256)
    down = packed[GU_ROWS:].reshape(DOWN_BLOCKS, DOWN_ROWS, PACK_COLS).transpose(1, 0, 2)
    return gu, down.reshape(1, DOWN_ROWS, -1)


def to_parts(packed):
    rows = packed.shape[0] // 4
    return packed.reshape(4, rows, 4, 128).transpose(0, 2, 1, 3).reshape(PIECES, rows, 128)


def from_parts(parts):
    rows = parts.shape[1]
    return parts.reshape(4, 4, rows, 128).transpose(0, 2, 1, 3).reshape(4 * rows, PACK_COLS)


def spread(parts):
    return lax.all_to_all(parts, "expert", split_axis=0, concat_axis=0, tiled=True)


def assemble_kernel(own, below, above, far_same, far_other, gu_ref, down_ref):
    me = lax.axis_index("dp")
    z, y = me // 2, lax.rem(me, 2)
    shards = [(0, own, 0), (0, own, 1), (3, below, 0), (3, below, 1), (1, above, 0), (1, above, 1)]
    shards += [(2, far_same, 0), (2, far_other, 1)]
    for dz, ref, dy in shards:
        shard = ref if dz == 2 else ref.at[dy]
        src = lax.rem(z + dz, 4) * 2 + lax.rem(y + dy, 2)
        gu_rows = pl.ds(pl.multiple_of(src * GU_ROWS, GU_ROWS), GU_ROWS)
        down_rows = pl.ds(pl.multiple_of(src * DOWN_ROWS, DOWN_ROWS), DOWN_ROWS)
        gu_ref[gu_rows, :] = shard[:GU_ROWS, :]
        for n in range(DOWN_BLOCKS):
            at = GU_ROWS + n * DOWN_ROWS
            down_ref[down_rows, n * PACK_COLS : (n + 1) * PACK_COLS] = shard[at : at + DOWN_ROWS, :]


def first_steps(shard):
    partner = lax.ppermute(shard, "dp", dp_shift(0, 1))
    own = jnp.stack([shard, partner])
    below = lax.ppermute(own, "dp", dp_shift(1, 0))
    above = lax.ppermute(own, "dp", dp_shift(3, 0))
    return own, below, above


def gather_dp(own, below, above, width, hidden_width):
    far_same = lax.ppermute(below[0], "dp", dp_shift(1, 0))
    far_other = lax.ppermute(above[1], "dp", dp_shift(3, 0))
    full = pl.pallas_call(
        assemble_kernel,
        out_shape=(
            jax.ShapeDtypeStruct((width, PACK_COLS), jnp.bfloat16),
            jax.ShapeDtypeStruct((hidden_width, width), jnp.bfloat16),
        ),
        in_specs=[pl.BlockSpec(memory_space=pltpu.VMEM)] * 5,
        out_specs=(pl.BlockSpec(memory_space=pltpu.VMEM),) * 2,
        compiler_params=pltpu.CompilerParams(vmem_limit_bytes=KERNEL_VMEM),
        name="assemble",
    )(own, below, above, far_same, far_other)
    return (*full, far_same, far_other)


def split_kernel(gu_ref, down_ref, own, above, below, far_same, far_other):
    me = lax.axis_index("dp")
    z, y = me // 2, lax.rem(me, 2)
    shards = [(0, own, 0), (0, own, 1), (1, above, 0), (1, above, 1), (3, below, 0), (3, below, 1)]
    shards += [(2, far_same, 0), (2, far_other, 1)]
    for dz, ref, dy in shards:
        shard = ref if dz == 2 else ref.at[dy]
        dst = lax.rem(z + dz, 4) * 2 + lax.rem(y + dy, 2)
        gu_rows = pl.ds(pl.multiple_of(dst * GU_ROWS, GU_ROWS), GU_ROWS)
        down_rows = pl.ds(pl.multiple_of(dst * DOWN_ROWS, DOWN_ROWS), DOWN_ROWS)
        shard[:GU_ROWS, :] = gu_ref[gu_rows, :]
        for n in range(DOWN_BLOCKS):
            at = GU_ROWS + n * DOWN_ROWS
            shard[at : at + DOWN_ROWS, :] = down_ref[down_rows, n * PACK_COLS : (n + 1) * PACK_COLS]


def split(grad_pair, grad_down):
    one = jax.ShapeDtypeStruct((PACK_ROWS, PACK_COLS), jnp.bfloat16)
    two = jax.ShapeDtypeStruct((2, PACK_ROWS, PACK_COLS), jnp.bfloat16)
    return pl.pallas_call(
        split_kernel,
        out_shape=(two, two, two, one, one),
        in_specs=[pl.BlockSpec(memory_space=pltpu.VMEM)] * 2,
        out_specs=(pl.BlockSpec(memory_space=pltpu.VMEM),) * 5,
        compiler_params=pltpu.CompilerParams(vmem_limit_bytes=KERNEL_VMEM),
        name="split",
    )(grad_pair, grad_down)


def add(term, other):
    return term.astype(jnp.float32) + other.astype(jnp.float32)


def join_kernel(above, below, far_same, far_other, above_out, below_out):
    for at in range(0, PACK_ROWS, 32):
        here = pl.ds(at, 32)
        above_out[0, here, :] = add(above[0, here, :], far_same[here, :]).astype(jnp.bfloat16)
        above_out[1, here, :] = above[1, here, :]
        below_out[0, here, :] = below[0, here, :]
        below_out[1, here, :] = add(below[1, here, :], far_other[here, :]).astype(jnp.bfloat16)


def join(above, below, far_same, far_other):
    return pl.pallas_call(
        join_kernel,
        out_shape=(jax.ShapeDtypeStruct(above.shape, above.dtype),) * 2,
        in_specs=[pl.BlockSpec(memory_space=pltpu.VMEM)] * 4,
        out_specs=(pl.BlockSpec(memory_space=pltpu.VMEM),) * 2,
        compiler_params=pltpu.CompilerParams(vmem_limit_bytes=KERNEL_VMEM),
        name="join",
    )(above, below, far_same, far_other)


def finish_kernel(own, above, below, other, parts, squares_out, total):
    rows = PACK_ROWS // 4
    squares = jnp.zeros((8, PACK_COLS), jnp.float32)
    for at in range(0, PACK_ROWS, 32):
        here = pl.ds(at, 32)
        value = add(own[0, here, :], above[0, here, :]) + add(below[0, here, :], other[here, :])
        total[here, :] = value
        squares = squares + jnp.sum((value * value).reshape(4, 8, PACK_COLS), axis=0)
    squares_out[...] = jnp.broadcast_to(jnp.sum(squares, keepdims=True), (8, 128))
    pad = jnp.zeros((8, 128), jnp.float32)
    for k in range(PIECES):
        value = total[pl.ds(k // 4 * rows, rows), pl.ds(k % 4 * 128, 128)]
        parts[k] = jnp.concatenate([value, pad], axis=0).astype(jnp.bfloat16)


def finish(own, above, below, other):
    return pl.pallas_call(
        finish_kernel,
        out_shape=(
            jax.ShapeDtypeStruct((PIECES, PACK_ROWS // 4 + 8, 128), jnp.bfloat16),
            jax.ShapeDtypeStruct((8, 128), jnp.float32),
        ),
        in_specs=[pl.BlockSpec(memory_space=pltpu.VMEM)] * 4,
        out_specs=(pl.BlockSpec(memory_space=pltpu.VMEM),) * 2,
        scratch_shapes=[pltpu.VMEM((PACK_ROWS, PACK_COLS), jnp.float32)],
        compiler_params=pltpu.CompilerParams(vmem_limit_bytes=KERNEL_VMEM),
        name="finish",
    )(own, above, below, other)


def regroup_kernel(place, parts, squares, out):
    left = squares[0:1, :]
    digits = []
    for _ in range(3):
        digit = left.astype(jnp.bfloat16).astype(jnp.float32)
        digits.append(digit)
        left = left - digit
    row = lax.broadcasted_iota(jnp.int32, (8, 128), 0)
    digits = jnp.where(row == 0, digits[0], jnp.where(row == 1, digits[1], digits[2]))
    for k in range(PIECES):
        value = parts[place[k]].astype(jnp.float32)[: PACK_ROWS // 4]
        out[k] = jnp.concatenate([value, digits], axis=0).astype(jnp.bfloat16)


def regroup(place, parts, squares):
    return pl.pallas_call(
        regroup_kernel,
        out_shape=jax.ShapeDtypeStruct(parts.shape, parts.dtype),
        in_specs=[
            pl.BlockSpec(memory_space=pltpu.SMEM),
            pl.BlockSpec(memory_space=pltpu.VMEM),
            pl.BlockSpec(memory_space=pltpu.VMEM),
        ],
        out_specs=pl.BlockSpec(memory_space=pltpu.VMEM),
        compiler_params=pltpu.CompilerParams(vmem_limit_bytes=KERNEL_VMEM),
        name="regroup",
    )(place, parts, squares)


def per_device(
    tokens,
    cotangent,
    expert_ids,
    gate_scale,
    old_place,
    new_place,
    gate_up,
    down_proj,
    first_gu,
    second_gu,
    first_down,
    second_down,
):
    experts = PIECES // HSPLIT
    tok_rows, width = tokens.shape
    hidden_width = down_proj.shape[1] * DP
    capacity = 3 * tok_rows // (2 * experts)
    numbers = jnp.arange(PIECES, dtype=jnp.int32)
    old_holder = jnp.sum(
        (old_place[None, :] == numbers[:, None]).astype(jnp.int32) * numbers[None, :], axis=1
    )
    source = old_holder[new_place]

    moments = jnp.concatenate(
        [
            to_parts(pack(first_gu, first_down).astype(jnp.bfloat16)),
            to_parts(pack(second_gu, second_down).astype(jnp.bfloat16)),
        ],
        axis=1,
    )
    weight_parts = spread(to_parts(pack(gate_up, down_proj)))
    shard = from_parts(spread(after(weight_parts, moments)[old_holder]))
    shards = first_steps(shard)

    chosen = expert_ids[:, 0]
    chosen = jnp.stack([chosen, lax.ppermute(chosen, "expert", YHI_SWAP)])
    hit_table = (chosen[:, :, None] == jnp.arange(experts, dtype=jnp.int32)).astype(jnp.int32)
    rank_in = jnp.sum((jnp.cumsum(hit_table, axis=1) - 1) * hit_table, axis=2)
    own_x = lax.axis_index("expert") // HSPLIT
    steps = (own_x - jnp.arange(experts, dtype=jnp.int32)) % experts

    def picker_of(codes, count):
        lanes = jnp.arange(count, dtype=jnp.int32)
        return (lanes[:, None] == codes.reshape(-1)[None, :]).astype(jnp.bfloat16)

    block = (chosen - own_x) % experts
    picker = picker_of(block[0] * capacity + rank_in[0], experts * capacity)
    expert_picker = picker_of(chosen[0] * capacity + rank_in[0], experts * capacity)
    halves = jnp.arange(2, dtype=jnp.int32)[:, None] * capacity
    home_picker = picker_of(block * 2 * capacity + halves + rank_in, experts * 2 * capacity)

    def pick(table, row_data):
        lined_up = jnp.dot(table, row_data, preferred_element_type=jnp.float32)
        return lined_up.astype(jnp.bfloat16).reshape(experts, capacity, width)

    def along_x(blocks, sign, *earlier):
        moved = [
            lax.ppermute(blocks[k], "expert", x_shift(sign * k)) for k in range(1, experts)
        ]
        moved = lax.optimization_barrier((*moved, *earlier))[: len(moved)]
        return jnp.concatenate([blocks[0], *moved], axis=0)

    def over_x(blocks):
        return lax.all_to_all(
            blocks, "expert", split_axis=0, concat_axis=0, axis_index_groups=X_GROUPS, tiled=True
        )

    def to_slices(own, *earlier):
        over_y = after(lax.ppermute(own, "expert", YHI_SWAP), *earlier)
        return (
            own,
            over_y,
            lax.ppermute(own, "expert", CORE_SWAP),
            lax.ppermute(over_y, "expert", CORE_SWAP),
        )

    def over_core(own_half, other_half):
        rows = add(own_half, lax.ppermute(other_half, "expert", CORE_SWAP)).astype(jnp.bfloat16)
        rows = rows.reshape(2, experts, capacity, width).transpose(1, 0, 2, 3)
        return rows.reshape(experts, 2 * capacity, width)

    def home_steps(blocks):
        moved = [lax.ppermute(blocks[k], "expert", x_shift(-k)) for k in range(1, experts)]
        return blocks[0], *moved

    def unpick(blocks):
        both = lax.dot_general(
            home_picker,
            jnp.concatenate(blocks, axis=0),
            (((0,), (0,)), ((), ())),
            preferred_element_type=jnp.float32,
        )
        theirs = lax.ppermute(both[tok_rows:].astype(jnp.bfloat16), "expert", YHI_SWAP)
        return both[:tok_rows], theirs

    scaled = (gate_scale[:, None] * cotangent.astype(jnp.float32)).astype(jnp.bfloat16)
    token_own = along_x(pick(picker, tokens), 1, shard)
    row_block = jnp.concatenate(to_slices(token_own), axis=0)
    cot_lanes = over_x(after(pick(expert_picker, scaled), shard))
    *shards, cot_lanes = lax.optimization_barrier((*shards, cot_lanes))
    gu_full, down_full, *last_steps = gather_dp(*shards, width, hidden_width)
    cot_rows = to_slices(cot_lanes[steps].reshape(-1, width), *last_steps)
    cot_block = jnp.concatenate(cot_rows, axis=0)
    moments = spread(after(moments, cot_rows[1]))

    hidden = jnp.dot(row_block, gu_full, preferred_element_type=jnp.float32)
    gate_half = hidden[:, :hidden_width]
    up_half = hidden[:, hidden_width:]
    sigmoid_val = jax.nn.sigmoid(gate_half)
    swish = gate_half * sigmoid_val
    activation = (swish * up_half).astype(jnp.bfloat16)
    back = lax.dot_general(
        cot_block, down_full, (((1,), (1,)), ((), ())), preferred_element_type=jnp.float32
    )
    slope = sigmoid_val * (1.0 + gate_half * (1.0 - sigmoid_val))
    dgu = jnp.concatenate([back * up_half * slope, back * swish], axis=1).astype(jnp.bfloat16)
    half = activation.shape[0] // 2

    def down_rows(rows):
        return jnp.dot(rows, down_full, preferred_element_type=jnp.float32).astype(jnp.bfloat16)

    def token_rows(rows):
        return lax.dot_general(
            rows, gu_full, (((1,), (1,)), ((), ())), preferred_element_type=jnp.float32
        ).astype(jnp.bfloat16)

    out_other, out_own = down_rows(activation[half:]), down_rows(activation[:half])
    dgu, out_other, out_own = lax.optimization_barrier((dgu, out_other, out_own))
    out_blocks = over_core(out_own, out_other)
    grad_down = lax.dot_general(
        activation, cot_block, (((0,), (0,)), ((), ())), preferred_element_type=jnp.float32
    ).astype(jnp.bfloat16)
    grad_pair = lax.dot_general(
        row_block, dgu, (((0,), (0,)), ((), ())), preferred_element_type=jnp.float32
    ).astype(jnp.bfloat16)
    own, above, below, far_same, far_other, dgu, moments = lax.optimization_barrier(
        (*split(grad_pair, grad_down), dgu, moments)
    )
    far_same = lax.ppermute(far_same, "dp", dp_shift(1, 0))
    far_other = lax.ppermute(far_other, "dp", dp_shift(3, 0))
    above, below = join(above, below, far_same, far_other)
    above, below, dgu, moments = lax.optimization_barrier((above, below, dgu, moments))
    above = lax.ppermute(above, "dp", dp_shift(1, 0))
    below = lax.ppermute(below, "dp", dp_shift(3, 0))
    state = spread(jnp.concatenate([weight_parts, moments], axis=1)[source])
    out_back = home_steps(out_blocks)
    token_back = home_steps(over_core(token_rows(dgu[:half]), token_rows(dgu[half:])))
    other_sum = (add(own[1], above[1]) + below[1].astype(jnp.float32)).astype(jnp.bfloat16)
    other_sum = after(other_sum, state, *out_back[1:])
    other_sum = lax.ppermute(other_sum, "dp", dp_shift(0, 1))
    grad_parts, squares = finish(own, above, below, other_sum)
    rows = PACK_ROWS // 4
    weight_now = from_parts(state[:, :rows]).astype(jnp.float32)
    first_now = from_parts(state[:, rows : 2 * rows]).astype(jnp.float32)
    second_now = from_parts(state[:, 2 * rows :]).astype(jnp.float32)

    squares = squares + lax.ppermute(squares, "dp", dp_flip(1, 0))
    out_home, out_theirs = unpick(lax.optimization_barrier((*out_back, squares))[:experts])
    for step in ((2, 0), (0, 1)):
        squares = squares + lax.ppermute(squares, "dp", dp_flip(*step))
    grad_parts = spread(grad_parts)
    token_back = lax.optimization_barrier((*token_back, grad_parts))[:experts]
    token_home, token_theirs = unpick(token_back)
    grad_parts = spread(regroup(new_place, grad_parts, squares))
    grad_now = from_parts(grad_parts[:, :rows]).astype(jnp.float32)
    total = jnp.sum(grad_parts[:, rows : rows + 3, 0].astype(jnp.float32))
    limit = 0.5 * jnp.sqrt(jnp.float32(3 * PIECES * width * hidden_width))
    clip_factor = jnp.minimum(1.0, limit / (jnp.sqrt(total) + 1e-06))

    output = (add(out_home, out_theirs) * gate_scale[:, None]).astype(jnp.bfloat16)
    token_grad = add(token_home, token_theirs).astype(jnp.bfloat16)

    scaled_grad = clip_factor * grad_now
    first_next = first_decay * first_now + (1.0 - first_decay) * scaled_grad
    second_next = second_decay * second_now + (1.0 - second_decay) * scaled_grad * scaled_grad
    weight_next = weight_now - learn_rate * first_next / (jnp.sqrt(second_next) + adam_epsilon)
    gu_next, down_next = unpack(weight_next.astype(jnp.bfloat16))
    first_gu_next, first_down_next = unpack(first_next)
    second_gu_next, second_down_next = unpack(second_next)
    return (
        output,
        token_grad,
        gu_next,
        down_next,
        first_gu_next,
        second_gu_next,
        first_down_next,
        second_down_next,
    )


def solution(mesh):
    rows = P(("dp", "expert"), None)
    gu, down = P("expert", "dp", None, None), P("expert", "dp", None)
    return jax.shard_map(
        per_device,
        mesh=mesh,
        in_specs=(rows, rows, rows, P(("dp", "expert")), P(), P(), gu, down, gu, gu, down, down),
        out_specs=(rows, rows, gu, down, gu, gu, down, down),
        check_vma=False,
    )
```

```python
import jax
import jax.numpy as jnp
from jax import lax
from jax.experimental import pallas as pl
from jax.experimental.pallas import tpu as pltpu
from jax.sharding import PartitionSpec as P

HSPLIT = 4
PIECES = 16
DP = 8
GU_ROWS = 448
DOWN_ROWS = 32
DOWN_BLOCKS = 7
PACK_ROWS = GU_ROWS + DOWN_ROWS * DOWN_BLOCKS
PACK_COLS = 512
KERNEL_VMEM = 32 * 1024 * 1024

first_decay = 0.9
second_decay = 0.95
learn_rate = 0.001
adam_epsilon = 1e-08

CORE_SWAP = [(i, i ^ 1) for i in range(16)]
YHI_SWAP = [(i, i ^ 2) for i in range(16)]


X_GROUPS = [[x * 4 + s for x in range(4)] for s in range(4)]


def x_shift(dx):
    return [(x * 4 + s, ((x + dx) % 4) * 4 + s) for x in range(4) for s in range(4)]


def dp_shift(dz, dy):
    return [(z * 2 + y, ((z + dz) % 4) * 2 + (y ^ dy)) for z in range(4) for y in range(2)]


def dp_flip(dz, dy):
    return [(i, i ^ (dz * 2 + dy)) for i in range(DP)]


def after(value, *earlier):
    return lax.optimization_barrier((value, *earlier))[0]


def pack(gu, down):
    rows = down.reshape(DOWN_ROWS, DOWN_BLOCKS, PACK_COLS).transpose(1, 0, 2)
    return jnp.concatenate([gu.reshape(GU_ROWS, PACK_COLS), rows.reshape(-1, PACK_COLS)], axis=0)


def unpack(packed):
    gu = packed[:GU_ROWS].reshape(1, GU_ROWS, 2, 256)
    down = packed[GU_ROWS:].reshape(DOWN_BLOCKS, DOWN_ROWS, PACK_COLS).transpose(1, 0, 2)
    return gu, down.reshape(1, DOWN_ROWS, -1)


def to_parts(packed):
    rows = packed.shape[0] // 4
    return packed.reshape(4, rows, 4, 128).transpose(0, 2, 1, 3).reshape(PIECES, rows, 128)


def from_parts(parts):
    rows = parts.shape[1]
    return parts.reshape(4, 4, rows, 128).transpose(0, 2, 1, 3).reshape(4 * rows, PACK_COLS)


def spread(parts):
    return lax.all_to_all(parts, "expert", split_axis=0, concat_axis=0, tiled=True)


def assemble_kernel(own, below, above, far_same, far_other, gu_ref, down_ref):
    me = lax.axis_index("dp")
    z, y = me // 2, lax.rem(me, 2)
    shards = [(0, own, 0), (0, own, 1), (3, below, 0), (3, below, 1), (1, above, 0), (1, above, 1)]
    shards += [(2, far_same, 0), (2, far_other, 1)]
    for dz, ref, dy in shards:
        shard = ref if dz == 2 else ref.at[dy]
        src = lax.rem(z + dz, 4) * 2 + lax.rem(y + dy, 2)
        gu_rows = pl.ds(pl.multiple_of(src * GU_ROWS, GU_ROWS), GU_ROWS)
        down_rows = pl.ds(pl.multiple_of(src * DOWN_ROWS, DOWN_ROWS), DOWN_ROWS)
        gu_ref[gu_rows, :] = shard[:GU_ROWS, :]
        for n in range(DOWN_BLOCKS):
            at = GU_ROWS + n * DOWN_ROWS
            down_ref[down_rows, n * PACK_COLS : (n + 1) * PACK_COLS] = shard[at : at + DOWN_ROWS, :]


def first_steps(shard):
    partner = lax.ppermute(shard, "dp", dp_shift(0, 1))
    own = jnp.stack([shard, partner])
    below = lax.ppermute(own, "dp", dp_shift(1, 0))
    above = lax.ppermute(own, "dp", dp_shift(3, 0))
    return own, below, above


def gather_dp(own, below, above, width, hidden_width):
    far_same = lax.ppermute(below[0], "dp", dp_shift(1, 0))
    far_other = lax.ppermute(above[1], "dp", dp_shift(3, 0))
    full = pl.pallas_call(
        assemble_kernel,
        out_shape=(
            jax.ShapeDtypeStruct((width, PACK_COLS), jnp.bfloat16),
            jax.ShapeDtypeStruct((hidden_width, width), jnp.bfloat16),
        ),
        in_specs=[pl.BlockSpec(memory_space=pltpu.VMEM)] * 5,
        out_specs=(pl.BlockSpec(memory_space=pltpu.VMEM),) * 2,
        compiler_params=pltpu.CompilerParams(vmem_limit_bytes=KERNEL_VMEM),
        name="assemble",
    )(own, below, above, far_same, far_other)
    return (*full, far_same, far_other)


def split_kernel(gu_ref, down_ref, own, above, below, far_same, far_other):
    me = lax.axis_index("dp")
    z, y = me // 2, lax.rem(me, 2)
    shards = [(0, own, 0), (0, own, 1), (1, above, 0), (1, above, 1), (3, below, 0), (3, below, 1)]
    shards += [(2, far_same, 0), (2, far_other, 1)]
    for dz, ref, dy in shards:
        shard = ref if dz == 2 else ref.at[dy]
        dst = lax.rem(z + dz, 4) * 2 + lax.rem(y + dy, 2)
        gu_rows = pl.ds(pl.multiple_of(dst * GU_ROWS, GU_ROWS), GU_ROWS)
        down_rows = pl.ds(pl.multiple_of(dst * DOWN_ROWS, DOWN_ROWS), DOWN_ROWS)
        shard[:GU_ROWS, :] = gu_ref[gu_rows, :]
        for n in range(DOWN_BLOCKS):
            at = GU_ROWS + n * DOWN_ROWS
            shard[at : at + DOWN_ROWS, :] = down_ref[down_rows, n * PACK_COLS : (n + 1) * PACK_COLS]


def split(grad_pair, grad_down):
    one = jax.ShapeDtypeStruct((PACK_ROWS, PACK_COLS), jnp.bfloat16)
    two = jax.ShapeDtypeStruct((2, PACK_ROWS, PACK_COLS), jnp.bfloat16)
    return pl.pallas_call(
        split_kernel,
        out_shape=(two, two, two, one, one),
        in_specs=[pl.BlockSpec(memory_space=pltpu.VMEM)] * 2,
        out_specs=(pl.BlockSpec(memory_space=pltpu.VMEM),) * 5,
        compiler_params=pltpu.CompilerParams(vmem_limit_bytes=KERNEL_VMEM),
        name="split",
    )(grad_pair, grad_down)


def add(term, other):
    return term.astype(jnp.float32) + other.astype(jnp.float32)


def join_kernel(above, below, far_same, far_other, above_out, below_out):
    for at in range(0, PACK_ROWS, 32):
        here = pl.ds(at, 32)
        above_out[0, here, :] = add(above[0, here, :], far_same[here, :]).astype(jnp.bfloat16)
        above_out[1, here, :] = above[1, here, :]
        below_out[0, here, :] = below[0, here, :]
        below_out[1, here, :] = add(below[1, here, :], far_other[here, :]).astype(jnp.bfloat16)


def join(above, below, far_same, far_other):
    return pl.pallas_call(
        join_kernel,
        out_shape=(jax.ShapeDtypeStruct(above.shape, above.dtype),) * 2,
        in_specs=[pl.BlockSpec(memory_space=pltpu.VMEM)] * 4,
        out_specs=(pl.BlockSpec(memory_space=pltpu.VMEM),) * 2,
        compiler_params=pltpu.CompilerParams(vmem_limit_bytes=KERNEL_VMEM),
        name="join",
    )(above, below, far_same, far_other)


def finish_kernel(own, above, below, other, parts, squares_out, total):
    rows = PACK_ROWS // 4
    squares = jnp.zeros((8, PACK_COLS), jnp.float32)
    for at in range(0, PACK_ROWS, 32):
        here = pl.ds(at, 32)
        value = add(own[0, here, :], above[0, here, :]) + add(below[0, here, :], other[here, :])
        total[here, :] = value
        squares = squares + jnp.sum((value * value).reshape(4, 8, PACK_COLS), axis=0)
    squares_out[...] = jnp.broadcast_to(jnp.sum(squares, keepdims=True), (8, 128))
    pad = jnp.zeros((8, 128), jnp.float32)
    for k in range(PIECES):
        value = total[pl.ds(k // 4 * rows, rows), pl.ds(k % 4 * 128, 128)]
        parts[k] = jnp.concatenate([value, pad], axis=0).astype(jnp.bfloat16)


def finish(own, above, below, other):
    return pl.pallas_call(
        finish_kernel,
        out_shape=(
            jax.ShapeDtypeStruct((PIECES, PACK_ROWS // 4 + 8, 128), jnp.bfloat16),
            jax.ShapeDtypeStruct((8, 128), jnp.float32),
        ),
        in_specs=[pl.BlockSpec(memory_space=pltpu.VMEM)] * 4,
        out_specs=(pl.BlockSpec(memory_space=pltpu.VMEM),) * 2,
        scratch_shapes=[pltpu.VMEM((PACK_ROWS, PACK_COLS), jnp.float32)],
        compiler_params=pltpu.CompilerParams(vmem_limit_bytes=KERNEL_VMEM),
        name="finish",
    )(own, above, below, other)


def regroup_kernel(place, parts, squares, out):
    left = squares[0:1, :]
    digits = []
    for _ in range(3):
        digit = left.astype(jnp.bfloat16).astype(jnp.float32)
        digits.append(digit)
        left = left - digit
    row = lax.broadcasted_iota(jnp.int32, (8, 128), 0)
    digits = jnp.where(row == 0, digits[0], jnp.where(row == 1, digits[1], digits[2]))
    for k in range(PIECES):
        value = parts[place[k]].astype(jnp.float32)[: PACK_ROWS // 4]
        out[k] = jnp.concatenate([value, digits], axis=0).astype(jnp.bfloat16)


def regroup(place, parts, squares):
    return pl.pallas_call(
        regroup_kernel,
        out_shape=jax.ShapeDtypeStruct(parts.shape, parts.dtype),
        in_specs=[
            pl.BlockSpec(memory_space=pltpu.SMEM),
            pl.BlockSpec(memory_space=pltpu.VMEM),
            pl.BlockSpec(memory_space=pltpu.VMEM),
        ],
        out_specs=pl.BlockSpec(memory_space=pltpu.VMEM),
        compiler_params=pltpu.CompilerParams(vmem_limit_bytes=KERNEL_VMEM),
        name="regroup",
    )(place, parts, squares)


def per_device(
    tokens,
    cotangent,
    expert_ids,
    gate_scale,
    old_place,
    new_place,
    gate_up,
    down_proj,
    first_gu,
    second_gu,
    first_down,
    second_down,
):
    experts = PIECES // HSPLIT
    tok_rows, width = tokens.shape
    hidden_width = down_proj.shape[1] * DP
    capacity = 3 * tok_rows // (2 * experts)
    numbers = jnp.arange(PIECES, dtype=jnp.int32)
    old_holder = jnp.sum(
        (old_place[None, :] == numbers[:, None]).astype(jnp.int32) * numbers[None, :], axis=1
    )
    source = old_holder[new_place]

    moments = jnp.concatenate(
        [
            to_parts(pack(first_gu, first_down).astype(jnp.bfloat16)),
            to_parts(pack(second_gu, second_down).astype(jnp.bfloat16)),
        ],
        axis=1,
    )
    weight_parts = spread(to_parts(pack(gate_up, down_proj)))
    shard = from_parts(spread(after(weight_parts, moments)[old_holder]))
    shards = first_steps(shard)

    chosen = expert_ids[:, 0]
    chosen = jnp.stack([chosen, lax.ppermute(chosen, "expert", YHI_SWAP)])
    hit_table = (chosen[:, :, None] == jnp.arange(experts, dtype=jnp.int32)).astype(jnp.int32)
    rank_in = jnp.sum((jnp.cumsum(hit_table, axis=1) - 1) * hit_table, axis=2)
    own_x = lax.axis_index("expert") // HSPLIT
    steps = (own_x - jnp.arange(experts, dtype=jnp.int32)) % experts

    def picker_of(codes, count):
        lanes = jnp.arange(count, dtype=jnp.int32)
        return (lanes[:, None] == codes.reshape(-1)[None, :]).astype(jnp.bfloat16)

    block = (chosen - own_x) % experts
    picker = picker_of(block[0] * capacity + rank_in[0], experts * capacity)
    expert_picker = picker_of(chosen[0] * capacity + rank_in[0], experts * capacity)
    halves = jnp.arange(2, dtype=jnp.int32)[:, None] * capacity
    home_picker = picker_of(block * 2 * capacity + halves + rank_in, experts * 2 * capacity)

    def pick(table, row_data):
        lined_up = jnp.dot(table, row_data, preferred_element_type=jnp.float32)
        return lined_up.astype(jnp.bfloat16).reshape(experts, capacity, width)

    def along_x(blocks, sign, *earlier):
        moved = [
            lax.ppermute(blocks[k], "expert", x_shift(sign * k)) for k in range(1, experts)
        ]
        moved = lax.optimization_barrier((*moved, *earlier))[: len(moved)]
        return jnp.concatenate([blocks[0], *moved], axis=0)

    def over_x(blocks):
        return lax.all_to_all(
            blocks, "expert", split_axis=0, concat_axis=0, axis_index_groups=X_GROUPS, tiled=True
        )

    def to_slices(own, *earlier):
        over_y = after(lax.ppermute(own, "expert", YHI_SWAP), *earlier)
        return (
            own,
            over_y,
            lax.ppermute(own, "expert", CORE_SWAP),
            lax.ppermute(over_y, "expert", CORE_SWAP),
        )

    def over_core(own_half, other_half):
        rows = add(own_half, lax.ppermute(other_half, "expert", CORE_SWAP)).astype(jnp.bfloat16)
        rows = rows.reshape(2, experts, capacity, width).transpose(1, 0, 2, 3)
        return rows.reshape(experts, 2 * capacity, width)

    def home_steps(blocks):
        moved = [lax.ppermute(blocks[k], "expert", x_shift(-k)) for k in range(1, experts)]
        return blocks[0], *moved

    def unpick(blocks):
        both = lax.dot_general(
            home_picker,
            jnp.concatenate(blocks, axis=0),
            (((0,), (0,)), ((), ())),
            preferred_element_type=jnp.float32,
        )
        theirs = lax.ppermute(both[tok_rows:].astype(jnp.bfloat16), "expert", YHI_SWAP)
        return both[:tok_rows], theirs

    scaled = (gate_scale[:, None] * cotangent.astype(jnp.float32)).astype(jnp.bfloat16)
    token_own = along_x(pick(picker, tokens), 1, shard)
    row_block = jnp.concatenate(to_slices(token_own), axis=0)
    cot_lanes = over_x(after(pick(expert_picker, scaled), shard))
    *shards, cot_lanes = lax.optimization_barrier((*shards, cot_lanes))
    gu_full, down_full, *last_steps = gather_dp(*shards, width, hidden_width)
    cot_rows = to_slices(cot_lanes[steps].reshape(-1, width), *last_steps)
    cot_block = jnp.concatenate(cot_rows, axis=0)
    moments = spread(after(moments, cot_rows[1]))

    hidden = jnp.dot(row_block, gu_full, preferred_element_type=jnp.float32)
    gate_half = hidden[:, :hidden_width]
    up_half = hidden[:, hidden_width:]
    sigmoid_val = jax.nn.sigmoid(gate_half)
    swish = gate_half * sigmoid_val
    activation = (swish * up_half).astype(jnp.bfloat16)
    back = lax.dot_general(
        cot_block, down_full, (((1,), (1,)), ((), ())), preferred_element_type=jnp.float32
    )
    slope = sigmoid_val * (1.0 + gate_half * (1.0 - sigmoid_val))
    dgu = jnp.concatenate([back * up_half * slope, back * swish], axis=1).astype(jnp.bfloat16)
    half = activation.shape[0] // 2

    def down_rows(rows):
        return jnp.dot(rows, down_full, preferred_element_type=jnp.float32).astype(jnp.bfloat16)

    def token_rows(rows):
        return lax.dot_general(
            rows, gu_full, (((1,), (1,)), ((), ())), preferred_element_type=jnp.float32
        ).astype(jnp.bfloat16)

    out_other, out_own = down_rows(activation[half:]), down_rows(activation[:half])
    dgu, out_other, out_own = lax.optimization_barrier((dgu, out_other, out_own))
    out_blocks = over_core(out_own, out_other)
    grad_down = lax.dot_general(
        activation, cot_block, (((0,), (0,)), ((), ())), preferred_element_type=jnp.float32
    ).astype(jnp.bfloat16)
    grad_pair = lax.dot_general(
        row_block, dgu, (((0,), (0,)), ((), ())), preferred_element_type=jnp.float32
    ).astype(jnp.bfloat16)
    own, above, below, far_same, far_other, dgu, moments = lax.optimization_barrier(
        (*split(grad_pair, grad_down), dgu, moments)
    )
    far_same = lax.ppermute(far_same, "dp", dp_shift(1, 0))
    far_other = lax.ppermute(far_other, "dp", dp_shift(3, 0))
    above, below = join(above, below, far_same, far_other)
    above, below, dgu, moments = lax.optimization_barrier((above, below, dgu, moments))
    above = lax.ppermute(above, "dp", dp_shift(1, 0))
    below = lax.ppermute(below, "dp", dp_shift(3, 0))
    state = spread(jnp.concatenate([weight_parts, moments], axis=1)[source])
    out_back = home_steps(out_blocks)
    token_back = home_steps(over_core(token_rows(dgu[:half]), token_rows(dgu[half:])))
    other_sum = (add(own[1], above[1]) + below[1].astype(jnp.float32)).astype(jnp.bfloat16)
    other_sum = after(other_sum, state)
    other_sum = lax.ppermute(other_sum, "dp", dp_shift(0, 1))
    grad_parts, squares = finish(own, above, below, other_sum)
    rows = PACK_ROWS // 4
    weight_now = from_parts(state[:, :rows]).astype(jnp.float32)
    first_now = from_parts(state[:, rows : 2 * rows]).astype(jnp.float32)
    second_now = from_parts(state[:, 2 * rows :]).astype(jnp.float32)

    for step in ((1, 0), (2, 0)):
        squares = squares + lax.ppermute(squares, "dp", dp_flip(*step))
    out_home, out_theirs = unpick(lax.optimization_barrier((*out_back, squares))[:experts])
    squares = squares + lax.ppermute(squares, "dp", dp_flip(0, 1))
    grad_parts = spread(grad_parts)
    token_back = lax.optimization_barrier((*token_back, grad_parts))[:experts]
    token_home, token_theirs = unpick(token_back)
    grad_parts = spread(regroup(new_place, grad_parts, squares))
    grad_now = from_parts(grad_parts[:, :rows]).astype(jnp.float32)
    total = jnp.sum(grad_parts[:, rows : rows + 3, 0].astype(jnp.float32))
    limit = 0.5 * jnp.sqrt(jnp.float32(3 * PIECES * width * hidden_width))
    clip_factor = jnp.minimum(1.0, limit / (jnp.sqrt(total) + 1e-06))

    output = (add(out_home, out_theirs) * gate_scale[:, None]).astype(jnp.bfloat16)
    token_grad = add(token_home, token_theirs).astype(jnp.bfloat16)

    scaled_grad = clip_factor * grad_now
    first_next = first_decay * first_now + (1.0 - first_decay) * scaled_grad
    second_next = second_decay * second_now + (1.0 - second_decay) * scaled_grad * scaled_grad
    weight_next = weight_now - learn_rate * first_next / (jnp.sqrt(second_next) + adam_epsilon)
    gu_next, down_next = unpack(weight_next.astype(jnp.bfloat16))
    first_gu_next, first_down_next = unpack(first_next)
    second_gu_next, second_down_next = unpack(second_next)
    return (
        output,
        token_grad,
        gu_next,
        down_next,
        first_gu_next,
        second_gu_next,
        first_down_next,
        second_down_next,
    )


def solution(mesh):
    rows = P(("dp", "expert"), None)
    gu, down = P("expert", "dp", None, None), P("expert", "dp", None)
    return jax.shard_map(
        per_device,
        mesh=mesh,
        in_specs=(rows, rows, rows, P(("dp", "expert")), P(), P(), gu, down, gu, gu, down, down),
        out_specs=(rows, rows, gu, down, gu, gu, down, down),
        check_vma=False,
    )
```
